32 devices in a mesh: gz: 2 (over x), gx: 4 (over z), gy: 4 (over y, core).
Axes of the slice: x: 2, y: 2, z: 4, core: 2. Of those that a mesh axis runs over, the one named last changes fastest.
Arguments:
- section_pixels: bfloat16 [2, 2048, 8192], P('gz', 'gy', 'gx'), may hold values from -6 to 6
- tissue: int32 [2, 64, 256], P('gz', 'gy', 'gx'), may hold values 0 or 1
- peak_offsets: int32 [2, 2, 64, 256], P(None, 'gz', 'gy', 'gx'), may hold values from -8 to 8
Outputs:
- relaxed: float32 [2, 2, 64, 256], P(None, 'gz', 'gy', 'gx')
- placed: float32 [2, 2, 64, 256], P(None, 'gz', 'gy', 'gx')
The draws below stay inside these ranges and needn't reach their ends.
All inputs are finite; a program needn't handle non-finite values. No bound on the sum of `tissue` on one device may be relied on, other than what follows from the above.
Results may differ from the reference program's by a relative error of at most 0.0003.
Values may be sent and summed in bfloat16 or wider, within the bound.
A program may use at most 128 MiB of HBM per device.

```python
import math
import jax
import jax.numpy as jnp
from jax import lax

PATCH = 64
REACH = 12
SPACING = 32
ITERS = 3
SECTIONS = 2
NYN = 64
NXN = 256
HEIGHT = 2048
WIDTH = 8192


def place_ends(drawn, rng, low, high):
    index_at = [jax.random.randint(jax.random.fold_in(rng, axis), (), 0, length) for axis, length in enumerate(drawn.shape)]
    widest = drawn.shape.index(max(drawn.shape))
    neighbour = index_at[:widest] + [(index_at[widest] + 1) % drawn.shape[widest]] + index_at[widest + 1:]
    return drawn.at[tuple(index_at)].set(low).at[tuple(neighbour)].set(high)


def shard_levels(own_key, shape, shards, low, high):
    def one(dim, parts):
        steps = jax.random.uniform(jax.random.fold_in(jax.random.fold_in(own_key, 6), dim), (parts,), jnp.float32, low / len(shards), high / len(shards))
        return jnp.repeat(jnp.exp(steps), shape[dim] // parts).reshape((-1,) + (1,) * (len(shape) - dim - 1))

    loudness = one(*shards[0])
    for cut in shards[1:]:
        loudness = loudness * one(*cut)
    return loudness


def normal_values(rng, shape, width, reach, cuts=(), held_as=jnp.bfloat16):
    gain = shard_levels(rng, shape, cuts, -0.22, 0.18) if cuts else 1.0
    values = jax.random.normal(rng, shape, jnp.float32) * width * gain
    return jnp.minimum(jnp.maximum(values, -reach), reach).astype(held_as)


def setup_inputs(seed: int = 0) -> dict:
    key_of = jax.random.split(jax.random.key(seed), 4)
    return {
        "section_pixels": normal_values(key_of[0], (SECTIONS, HEIGHT, WIDTH), 1.0, 6.0, ((0, 2), (1, 4), (2, 4))),
        "tissue": place_ends((jax.random.randint(key_of[1], (SECTIONS, NYN, NXN), 0, 4) < 3).astype(jnp.int32), jax.random.fold_in(key_of[1], 1), 0, 1),
        "peak_offsets": place_ends(jax.random.randint(key_of[2], (2, SECTIONS, NYN, NXN), -8, 9), jax.random.fold_in(key_of[2], 1), -8, 8).astype(jnp.int32),
    }


sharpness = 32.0
tiny_energy = 1e-06

def phase_tables(length):
    frequency = jnp.arange(length, dtype=jnp.int32)
    angles = jnp.mod(frequency[:, None] * frequency[None, :], length).astype(jnp.float32) * (2.0 * math.pi / length)
    cosine = jnp.cos(angles)
    sine_part = jnp.sin(angles)
    first_table = jnp.concatenate([cosine, -sine_part], 0).astype(jnp.bfloat16)
    second_table = jnp.stack([jnp.stack([cosine, sine_part], 0), jnp.stack([-sine_part, cosine], 0)], 0).astype(jnp.bfloat16)
    return (first_table, second_table)

def cut_patches(section, node_rows, node_cols):
    blocks = section.reshape(node_rows + 1, SPACING, node_cols + 1, SPACING)
    quarters = [jnp.stack([blocks[row_half:row_half + node_rows, :, col_half:col_half + node_cols, :] for col_half in (0, 1)], 0) for row_half in (0, 1)]
    stacked = jnp.stack(quarters, 0)
    ordered = jnp.transpose(stacked, (0, 3, 1, 5, 2, 4))
    return ordered.reshape(PATCH, PATCH, node_rows * node_cols)

def spectrum(patches, first_table, second_table):
    patch_count = patches.shape[2]
    flattened = patches.reshape(PATCH, PATCH * patch_count)
    half_spec = jnp.dot(first_table, flattened, preferred_element_type=jnp.float32).astype(jnp.bfloat16)
    half_spec = lax.optimization_barrier(half_spec)
    half_spec = half_spec.reshape(2, PATCH, PATCH, patch_count).astype(jnp.float32)
    return jnp.einsum('okxc,kycp->oyxp', second_table.astype(jnp.float32), half_spec, precision=lax.Precision.HIGHEST)

def phase_of(values):
    frequency = jnp.arange(PATCH, dtype=jnp.int32).reshape((PATCH,) + (1,) * values.ndim)
    angles = jnp.mod(frequency * values[None], PATCH).astype(jnp.float32) * (2.0 * math.pi / PATCH)
    return (jnp.cos(angles), jnp.sin(angles))

def match_patches(spec_a, energy_a, spec_b, energy_b, offset_pair, living):
    highest = lax.Precision.HIGHEST
    cross_real = spec_a[0] * spec_b[0] + spec_a[1] * spec_b[1]
    cross_imag = spec_a[0] * spec_b[1] - spec_a[1] * spec_b[0]
    row_cos, row_sin = phase_of(offset_pair[0])
    col_cos, col_sin = phase_of(offset_pair[1])
    turn_cosine = row_cos[:, None, :] * col_cos[None] - row_sin[:, None, :] * col_sin[None]
    turn_sine = row_sin[:, None, :] * col_cos[None] + row_cos[:, None, :] * col_sin[None]
    rotated = jnp.stack([cross_real * turn_cosine - cross_imag * turn_sine, cross_real * turn_sine + cross_imag * turn_cosine], 0)
    lag_count = 2 * REACH + 1
    lag_values = jnp.arange(lag_count, dtype=jnp.int32) - REACH
    lag_cos, lag_sin = phase_of(lag_values)
    row_lag_table = jnp.stack([jnp.stack([lag_cos, -lag_sin], 0), jnp.stack([lag_sin, lag_cos], 0)], 0)
    col_lag_table = jnp.stack([lag_cos, -lag_sin], 0)
    first_pass = jnp.einsum('kfgp,jkfe->jegp', rotated, row_lag_table, precision=highest)
    correlation = jnp.einsum('jegp,jgh->ehp', first_pass, col_lag_table, precision=highest) / float(PATCH * PATCH)
    likeness = correlation / jnp.sqrt(energy_a * energy_b + tiny_energy)
    weights = jnp.exp(sharpness * likeness)
    weight_sum = lax.optimization_barrier(jnp.sum(weights, axis=(0, 1)))
    lag_steps = lag_values.astype(jnp.float32)
    row_shift = lax.optimization_barrier(jnp.sum(weights * lag_steps[:, None, None], axis=(0, 1))) / weight_sum
    col_shift = lax.optimization_barrier(jnp.sum(weights * lag_steps[None, :, None], axis=(0, 1))) / weight_sum
    target = jnp.stack([offset_pair[0].astype(jnp.float32) + row_shift, offset_pair[1].astype(jnp.float32) + col_shift], 0)
    stiffness = living * weight_sum / float(lag_count * lag_count)
    return (target, stiffness)

def neighbour_sum(padded):
    return padded[..., :-2, 1:-1] + padded[..., 2:, 1:-1] + padded[..., 1:-1, :-2] + padded[..., 1:-1, 2:]

def pad_nodes(field):
    widths = [(0, 0)] * (field.ndim - 2) + [(1, 1), (1, 1)]
    return jnp.pad(field, widths)

def relax_update(moved, living, stiffness, target, living_padded, moved_padded):
    neighbours = neighbour_sum(living_padded)
    pulled = neighbour_sum(living_padded[None] * moved_padded)
    numerator = moved + stiffness[None] * target + living[None] * pulled
    return numerator / (1.0 + stiffness + living * neighbours)[None]

def reference(section_pixels, tissue, peak_offsets):
    first_table, second_table = phase_tables(PATCH)
    margin = SPACING // 2
    closing = jnp.zeros((1, HEIGHT, WIDTH), jnp.bfloat16)
    padded = jnp.pad(jnp.concatenate([section_pixels, closing], 0), ((0, 0), (margin, margin), (margin, margin)))
    patch_count = NYN * NXN

    def prepare(section):
        patches = cut_patches(section, NYN, NXN)
        energy = lax.optimization_barrier(jnp.sum(jnp.square(patches.astype(jnp.float32)), axis=(0, 1)))
        return (spectrum(patches, first_table, second_table), energy)
    opening = prepare(padded[0])
    offset_rows = jnp.transpose(peak_offsets.reshape(2, SECTIONS, patch_count), (1, 0, 2))
    living_rows = tissue.reshape(SECTIONS, patch_count).astype(jnp.float32)

    def advance(previous, inputs):
        section, offset_pair, living_row = inputs
        current = prepare(section)
        target, stiffness = match_patches(previous[0], previous[1], current[0], current[1], offset_pair, living_row)
        return (current, (target, stiffness))
    _, (targets, stiffs) = lax.scan(advance, opening, (padded[1:], offset_rows, living_rows))
    target = jnp.transpose(targets, (1, 0, 2)).reshape(2, SECTIONS, NYN, NXN)
    stiffness = stiffs.reshape(SECTIONS, NYN, NXN)
    living = tissue.astype(jnp.float32)
    moved = living[None] * target
    for sweep_index in range(ITERS):
        moved = relax_update(moved, living, stiffness, target, pad_nodes(living), pad_nodes(moved))
    return (moved, jnp.cumsum(moved, axis=1))
```

```python
import functools
import math

import jax
import jax.numpy as jnp
import ml_dtypes
import numpy as np
from jax import lax
from jax.experimental import pallas as pl
from jax.experimental.pallas import tpu as pltpu
from jax.sharding import PartitionSpec as P

PATCH = 64
REACH = 12
SPACING = 32
ITERS = 3
BOUND = 8
FAR = BOUND + REACH
LAG_ROWS = 48
HALF = PATCH // 2

sharpness = 32.0
tiny_energy = 1e-06


def bf16(table):
    return np.asarray(table, np.float32).astype(ml_dtypes.bfloat16)


def split(table):
    high = bf16(table)
    return high, bf16(np.asarray(table, np.float32) - high.astype(np.float32))


@functools.lru_cache(None)
def tables():
    n = np.arange(PATCH)
    angle = 2.0 * math.pi * ((n[:, None] * n[None, :]) % PATCH) / PATCH
    cosine, sine = np.cos(angle), np.sin(angle)
    row_table = np.zeros((80, PATCH))
    row_table[:HALF] = cosine[:HALF]
    row_table[HALF:PATCH] = -sine[:HALF]
    row_table[PATCH] = cosine[HALF]
    second = np.zeros((2, 256, 2, 2, 2, PATCH))
    spread = np.zeros((256, 4, PATCH))
    for pair in range(2):
        for q in range(2):
            node = 2 * pair + q
            rows = slice(SPACING * node, SPACING * node + PATCH)
            second[0, rows, pair, 0, q] = cosine.T
            second[0, rows, pair, 1, q] = -sine.T
            second[1, rows, pair, 0, q] = sine.T
            second[1, rows, pair, 1, q] = cosine.T
            spread[rows, node] = 1.0
    lags = np.arange(2 * FAR + 1) - FAR
    lag_angle = 2.0 * math.pi * ((n[:, None] * lags[None, :]) % PATCH) / PATCH
    lag_cos, lag_sin = np.cos(lag_angle), np.sin(lag_angle)
    back = np.zeros((2, 2, PATCH, 2, 2, PATCH))
    for q in range(2):
        back[0, q, :, 0, q, : lags.size] = lag_cos
        back[1, q, :, 0, q, : lags.size] = -lag_sin
        back[0, q, :, 1, q, : lags.size] = lag_sin
        back[1, q, :, 1, q, : lags.size] = lag_cos
    back_high, back_low = split(back.reshape(256, 256))
    fold = np.where(np.arange(HALF) == 0, 1.0, 2.0)[None]
    rows = np.zeros((LAG_ROWS, 2 * HALF))
    rows[: lags.size, :HALF] = fold * lag_cos[:HALF].T
    rows[: lags.size, HALF:] = -fold * lag_sin[:HALF].T
    row_high, row_low = split(rows)
    row_back = np.concatenate([row_high, row_high, row_low], 1)
    gather = np.zeros((2, 4, PATCH, 128))
    lane_lag = np.arange(PATCH) - FAR
    for node in range(4):
        gather[0, node, :, node] = 1.0
        gather[0, node, :, 4 + node] = lane_lag
        gather[1, node, :, 8 + node] = 1.0
    return (
        bf16(row_table),
        bf16(second.reshape(2, 256, 512)),
        np.asarray(spread.reshape(256, 256), np.float32),
        back_high,
        back_low,
        row_back,
        np.asarray(gather.reshape(2, 256, 128), np.float32),
    )


def match_kernel(
    node_rows,
    sign_ref,
    mine_ref,
    theirs_ref,
    offsets_ref,
    row_ref,
    second_ref,
    spread_ref,
    back_high_ref,
    back_low_ref,
    row_back_ref,
    gather_ref,
    out_ref,
    half_ref,
    nyquist_ref,
    squares_ref,
):
    f32, b16 = jnp.float32, jnp.bfloat16
    step = pl.program_id(0)

    def dot(a, b):
        return jnp.dot(a, b, preferred_element_type=f32)

    def exact(a, b):
        return jnp.dot(a, b, preferred_element_type=f32, precision=lax.Precision.HIGHEST)

    @pl.when(step == 0)
    def _():
        def one(i, _):
            for which, image in enumerate((mine_ref, theirs_ref)):
                rows = image[pl.ds(pl.multiple_of(i * SPACING, SPACING), PATCH), :]
                got = dot(row_ref[...], rows)
                at = pl.ds(pl.multiple_of(i * HALF, HALF), HALF)
                half_ref[which, 0, at, :] = got[:HALF].astype(b16)
                half_ref[which, 1, at, :] = got[HALF:PATCH].astype(b16)
                nyquist_ref[which, pl.ds(i, 1), :] = got[PATCH : PATCH + 1].astype(b16).astype(f32)
                wide = rows.astype(f32)
                squares_ref[which, pl.ds(i, 1), :] = jnp.sum(wide * wide, axis=0, keepdims=True)
            return 0

        lax.fori_loop(0, node_rows, one, 0)

    lanes = pl.ds(pl.multiple_of(step * 128, 128), 256)
    sign = sign_ref[0]
    spectra, edges, energies = [], [], []
    for which in range(2):
        spectra.append(
            dot(half_ref[which, 0, :, lanes], second_ref[0])
            + dot(half_ref[which, 1, :, lanes], second_ref[1])
        )
        edges.append(dot(nyquist_ref[which, :, lanes].astype(b16), second_ref[0]))
        energies.append(exact(squares_ref[which, :, lanes], spread_ref[...]))
    scale = (sharpness / (PATCH * PATCH)) / jnp.sqrt(energies[0] * energies[1] + tiny_energy)

    def over_columns(first, then, pair):
        real, imag = slice(256 * pair, 256 * pair + 128), slice(256 * pair + 128, 256 * pair + 256)
        cross_real = first[:, real] * then[:, real] + first[:, imag] * then[:, imag]
        cross_imag = sign * (first[:, real] * then[:, imag] - first[:, imag] * then[:, real])
        cross = jnp.concatenate([cross_real, cross_imag], 1)
        high = cross.astype(b16)
        low = (cross - high.astype(f32)).astype(b16)
        return dot(high, back_high_ref[...]) + dot(low, back_high_ref[...]) + dot(high, back_low_ref[...])

    columns = [over_columns(spectra[0], spectra[1], pair) for pair in range(2)]
    edge_columns = jnp.concatenate(
        [over_columns(edges[0], edges[1], pair)[:, :128] for pair in range(2)], 1
    )
    row_lag = lax.broadcasted_iota(jnp.int32, (LAG_ROWS, 256), 0) - FAR
    col_lag = (lax.broadcasted_iota(jnp.int32, (LAG_ROWS, 256), 1) & (PATCH - 1)) - FAR
    alternate = jnp.where((row_lag & 1) == 0, 1.0, -1.0).astype(f32)
    row_lag = row_lag.astype(f32)
    col_lag = col_lag.astype(f32)
    totals, row_totals = [], []
    for i in range(node_rows):
        rows = slice(i * HALF, (i + 1) * HALF)
        field = jnp.concatenate(
            [
                jnp.concatenate([columns[0][rows, :128], columns[1][rows, :128]], 1),
                jnp.concatenate([columns[0][rows, 128:], columns[1][rows, 128:]], 1),
            ],
            0,
        )
        high = field.astype(b16)
        low = (field - high.astype(f32)).astype(b16)
        found = dot(row_back_ref[...], jnp.concatenate([high, low, high], 0))
        found = found + alternate * edge_columns[i : i + 1]
        inside = (jnp.abs(row_lag - offsets_ref[0, i : i + 1, :]) <= REACH) & (
            jnp.abs(col_lag - offsets_ref[1, i : i + 1, :]) <= REACH
        )
        weights = jnp.where(inside, jnp.exp(found * scale[i : i + 1]), 0.0)
        totals.append(jnp.sum(weights, axis=0, keepdims=True))
        row_totals.append(jnp.sum(weights * row_lag, axis=0, keepdims=True))
    out_ref[0] = exact(jnp.concatenate(totals, 0), gather_ref[0]) + exact(
        jnp.concatenate(row_totals, 0), gather_ref[1]
    )


def match(mine, theirs, sign, offsets):
    node_rows, node_cols = offsets.shape[1:]
    groups = node_cols // 4
    width = mine.shape[1]
    constants = [jnp.asarray(table) for table in tables()]
    spread_offsets = jnp.repeat(offsets.astype(jnp.float32), PATCH, axis=2)
    whole = lambda a: pl.BlockSpec(a.shape, lambda m, n=a.ndim: (0,) * n)
    out = pl.pallas_call(
        functools.partial(match_kernel, node_rows),
        grid=(groups,),
        out_shape=jax.ShapeDtypeStruct((groups, node_rows, 128), jnp.float32),
        in_specs=[
            pl.BlockSpec(memory_space=pltpu.SMEM),
            whole(mine),
            whole(theirs),
            pl.BlockSpec((2, node_rows, 256), lambda m: (0, 0, m)),
        ]
        + [whole(table) for table in constants],
        out_specs=pl.BlockSpec((1, node_rows, 128), lambda m: (m, 0, 0)),
        scratch_shapes=[
            pltpu.VMEM((2, 2, node_rows * HALF, width), jnp.bfloat16),
            pltpu.VMEM((2, node_rows, width), jnp.float32),
            pltpu.VMEM((2, node_rows, width), jnp.float32),
        ],
        compiler_params=pltpu.CompilerParams(vmem_limit_bytes=56 * 1024 * 1024),
    )(sign, mine, theirs, spread_offsets, *constants)
    sums = jnp.transpose(out[:, :, :12].reshape(groups, node_rows, 3, 4), (2, 1, 0, 3))
    sums = sums.reshape(3, node_rows, node_cols)
    return jnp.stack([sums[2] / sums[0], sums[1] / sums[0], sums[0]], 0)


def beside(value, axis, steps):
    count = lax.axis_size(axis)
    pairs = [(i, i + steps) for i in range(count) if 0 <= i + steps < count]
    return lax.ppermute(value, axis, pairs)


def bordered(field, axis, dim, width):
    length = field.shape[dim]
    before = beside(lax.slice_in_dim(field, length - width, length, axis=dim), axis, 1)
    after = beside(lax.slice_in_dim(field, 0, width, axis=dim), axis, -1)
    return before, after


def neighbour_sum(padded):
    return (
        padded[..., :-2, 1:-1]
        + padded[..., 2:, 1:-1]
        + padded[..., 1:-1, :-2]
        + padded[..., 1:-1, 2:]
    )


def relax(target, stiffness, living):
    fields = jnp.concatenate([target, stiffness[None], living[None]], 0)
    before, after = bordered(fields, "gx", 3, ITERS)
    fields = jnp.concatenate([before, fields, after], 3)
    before, after = bordered(fields, "gy", 2, ITERS)
    fields = jnp.concatenate([before, fields, after], 2)
    target, stiffness, living = fields[:2], fields[2], fields[3]
    moved = living[None] * target
    for _ in range(ITERS):
        pulled = neighbour_sum(living[None] * moved)
        count = neighbour_sum(living)
        inner = (slice(None), slice(1, -1), slice(1, -1))
        target, moved = target[(slice(None),) + inner], moved[(slice(None),) + inner]
        stiffness, living = stiffness[inner], living[inner]
        moved = (moved + stiffness[None] * target + living[None] * pulled) / (
            1.0 + stiffness + living * count
        )[None]
    return moved


def shards(section_pixels, tissue, peak_offsets):
    margin = SPACING // 2
    own = section_pixels[0]
    pixel_rows, pixel_cols = own.shape
    node_rows = pixel_rows // SPACING
    slabs = lax.axis_size("gz")
    place = lax.axis_index("gz")
    before, after = bordered(own, "gx", 1, margin)
    spare = jnp.zeros((pixel_rows, 128 - 2 * margin), own.dtype)
    own = jnp.concatenate([before, own, after, spare], 1)
    before, after = bordered(own, "gy", 0, margin)
    own = jnp.concatenate([before, own, after], 0)
    offsets = peak_offsets[:, 0].astype(jnp.float32)
    living = tissue.astype(jnp.float32)
    per_node = jnp.float32((2 * REACH + 1) ** 2)

    if slabs == 2 and node_rows % 16 == 0:
        half_rows = node_rows // 2
        strip = half_rows * SPACING + SPACING
        swap = [(0, 1), (1, 0)]
        first = place == 0
        theirs = lax.ppermute(
            lax.dynamic_slice_in_dim(own, (1 - place) * (half_rows * SPACING), strip, 0), "gz", swap
        )
        mine = lax.dynamic_slice_in_dim(own, place * (half_rows * SPACING), strip, 0)
        nodes = jnp.concatenate([offsets, living], 0)
        other_nodes = lax.ppermute(nodes, "gz", swap)
        nodes_0 = jnp.where(first, nodes, other_nodes)
        nodes_1 = jnp.where(first, other_nodes, nodes)
        sign = jnp.where(first, 1.0, -1.0).astype(jnp.float32).reshape(1)
        ours = match(
            mine, theirs, sign, lax.dynamic_slice_in_dim(nodes_0[:2], place * half_rows, half_rows, 1)
        )
        others = lax.ppermute(ours, "gz", swap)
        matched = jnp.concatenate(
            [jnp.where(first, ours, others), jnp.where(first, others, ours)], 1
        )
        target = jnp.stack([matched[:2], nodes_1[:2]], 1)
        alive = jnp.stack([nodes_0[2], nodes_1[2]], 0)
        stiffness = jnp.stack([nodes_0[2] * matched[2] / per_node, nodes_1[2]], 0)
        moved = relax(target, stiffness, alive)
        relaxed = jnp.where(first, moved[:, 0], moved[:, 1])
        placed = jnp.where(first, moved[:, 0], moved[:, 0] + moved[:, 1])
        return relaxed[:, None], placed[:, None]

    theirs = beside(own, "gz", -1)
    matched = match(own, theirs, jnp.ones((1,), jnp.float32), offsets)
    moved = relax(matched[:2, None], living * matched[2:] / per_node, living)
    placed = moved
    reach = 1
    while reach < slabs:
        placed = placed + beside(placed, "gz", reach)
        reach *= 2
    return moved, placed


def solution(mesh):
    placed = (P("gz", "gy", "gx"), P("gz", "gy", "gx"), P(None, "gz", "gy", "gx"))
    return jax.shard_map(
        shards,
        mesh=mesh,
        in_specs=placed,
        out_specs=(P(None, "gz", "gy", "gx"), P(None, "gz", "gy", "gx")),
        check_vma=False,
    )
```

```python
import functools
import math

import jax
import jax.numpy as jnp
import ml_dtypes
import numpy as np
from jax import lax
from jax.experimental import pallas as pl
from jax.experimental.pallas import tpu as pltpu
from jax.sharding import PartitionSpec as P

PATCH = 64
REACH = 12
SPACING = 32
ITERS = 3
BOUND = 8
FAR = BOUND + REACH
LAG_ROWS = 48
HALF = PATCH // 2
MARGIN = SPACING // 2
LANES = 128
BLOCK = 256
MESH = pl.DeviceIdType.MESH

sharpness = 32.0
tiny_energy = 1e-06


def bf16(table):
    return np.asarray(table, np.float32).astype(ml_dtypes.bfloat16)


def split(table):
    high = bf16(table)
    return high, bf16(np.asarray(table, np.float32) - high.astype(np.float32))


@functools.lru_cache(None)
def tables():
    n = np.arange(PATCH)
    angle = 2.0 * math.pi * ((n[:, None] * n[None, :]) % PATCH) / PATCH
    cosine, sine = np.cos(angle), np.sin(angle)
    row_table = np.zeros((80, PATCH))
    row_table[:HALF] = cosine[:HALF]
    row_table[HALF:PATCH] = -sine[:HALF]
    row_table[PATCH] = cosine[HALF]
    second = np.zeros((2, 256, 2, 2, 2, PATCH))
    spread = np.zeros((256, 4, PATCH))
    for pair in range(2):
        for q in range(2):
            node = 2 * pair + q
            rows = slice(MARGIN + SPACING * node, MARGIN + SPACING * node + PATCH)
            second[0, rows, pair, 0, q] = cosine.T
            second[0, rows, pair, 1, q] = -sine.T
            second[1, rows, pair, 0, q] = sine.T
            second[1, rows, pair, 1, q] = cosine.T
            spread[rows, node] = 1.0
    lags = np.arange(2 * FAR + 1) - FAR
    lag_angle = 2.0 * math.pi * ((n[:, None] * lags[None, :]) % PATCH) / PATCH
    lag_cos, lag_sin = np.cos(lag_angle), np.sin(lag_angle)
    back = np.zeros((2, 2, PATCH, 2, 2, PATCH))
    for q in range(2):
        back[0, q, :, 0, q, : lags.size] = lag_cos
        back[1, q, :, 0, q, : lags.size] = -lag_sin
        back[0, q, :, 1, q, : lags.size] = lag_sin
        back[1, q, :, 1, q, : lags.size] = lag_cos
    back_high, back_low = split(back.reshape(256, 256))
    fold = np.where(np.arange(HALF) == 0, 1.0, 2.0)[None]
    rows = np.zeros((LAG_ROWS, 2 * HALF))
    rows[: lags.size, :HALF] = fold * lag_cos[:HALF].T
    rows[: lags.size, HALF:] = -fold * lag_sin[:HALF].T
    row_high, row_low = split(rows)
    row_back = np.concatenate([row_high, row_high, row_low], 1)
    gather = np.zeros((2, 4, PATCH, 128))
    lane_lag = np.arange(PATCH) - FAR
    for node in range(4):
        gather[0, node, :, node] = 1.0
        gather[0, node, :, 4 + node] = lane_lag
        gather[1, node, :, 8 + node] = 1.0
    return (
        bf16(row_table),
        bf16(second.reshape(2, 256, 512)),
        np.asarray(spread.reshape(256, 256), np.float32),
        back_high,
        back_low,
        row_back,
        np.asarray(gather.reshape(2, 256, 128), np.float32),
    )


def match_core(
    node_rows,
    strips_ref,
    offsets_ref,
    row_ref,
    second_ref,
    spread_ref,
    back_high_ref,
    back_low_ref,
    row_back_ref,
    gather_ref,
    out_ref,
    half_ref,
    nyquist_ref,
    squares_ref,
    arrive,
):
    f32, b16 = jnp.float32, jnp.bfloat16
    blocks = strips_ref.shape[2] // BLOCK

    def dot(a, b):
        return jnp.dot(a, b, preferred_element_type=f32)

    def exact(a, b):
        return jnp.dot(a, b, preferred_element_type=f32, precision=lax.Precision.HIGHEST)

    def over_rows(block):
        lanes = pl.ds(pl.multiple_of(block * BLOCK, BLOCK), BLOCK)
        for which in range(2):
            for i in range(node_rows):
                rows = strips_ref[which, i * SPACING : i * SPACING + PATCH, lanes]
                got = dot(row_ref[...], rows)
                half_ref[which, 0, i * HALF : (i + 1) * HALF, lanes] = got[:HALF].astype(b16)
                half_ref[which, 1, i * HALF : (i + 1) * HALF, lanes] = got[HALF:PATCH].astype(b16)
                nyquist_ref[which, i : i + 1, lanes] = (
                    got[PATCH : PATCH + 1].astype(b16).astype(f32)
                )
                wide = rows.astype(f32)
                squares_ref[which, i : i + 1, lanes] = jnp.sum(wide * wide, axis=0, keepdims=True)

    row_lag = lax.broadcasted_iota(jnp.int32, (LAG_ROWS, BLOCK), 0) - FAR
    col_lag = (lax.broadcasted_iota(jnp.int32, (LAG_ROWS, BLOCK), 1) & (PATCH - 1)) - FAR
    alternate = jnp.where((row_lag & 1) == 0, 1.0, -1.0).astype(f32)
    row_lag = row_lag.astype(f32)
    col_lag = col_lag.astype(f32)

    def over_columns(first, then, pair):
        real, imag = slice(256 * pair, 256 * pair + 128), slice(256 * pair + 128, 256 * pair + 256)
        cross_real = first[:, real] * then[:, real] + first[:, imag] * then[:, imag]
        cross_imag = first[:, real] * then[:, imag] - first[:, imag] * then[:, real]
        cross = jnp.concatenate([cross_real, cross_imag], 1)
        high = cross.astype(b16)
        low = (cross - high.astype(f32)).astype(b16)
        return dot(high, back_high_ref[...]) + dot(low, back_high_ref[...]) + dot(high, back_low_ref[...])

    def four_columns(group):
        lanes = pl.ds(pl.multiple_of((group + 1) * LANES, LANES), BLOCK)
        spectra, edges, energies = [], [], []
        for which in range(2):
            spectra.append(
                dot(half_ref[which, 0, :, lanes], second_ref[0])
                + dot(half_ref[which, 1, :, lanes], second_ref[1])
            )
            edges.append(dot(nyquist_ref[which, :, lanes].astype(b16), second_ref[0]))
            energies.append(exact(squares_ref[which, :, lanes], spread_ref[...]))
        scale = (sharpness / (PATCH * PATCH)) / jnp.sqrt(energies[0] * energies[1] + tiny_energy)
        columns = [over_columns(spectra[0], spectra[1], pair) for pair in range(2)]
        edge_columns = jnp.concatenate(
            [over_columns(edges[0], edges[1], pair)[:, :128] for pair in range(2)], 1
        )
        here = pl.ds(pl.multiple_of(group * BLOCK, BLOCK), BLOCK)
        row_offset = offsets_ref[0, :, here]
        col_offset = offsets_ref[1, :, here]
        totals, row_totals = [], []
        for i in range(node_rows):
            rows = slice(i * HALF, (i + 1) * HALF)
            field = jnp.concatenate(
                [
                    jnp.concatenate([columns[0][rows, :128], columns[1][rows, :128]], 1),
                    jnp.concatenate([columns[0][rows, 128:], columns[1][rows, 128:]], 1),
                ],
                0,
            )
            high = field.astype(b16)
            low = (field - high.astype(f32)).astype(b16)
            found = dot(row_back_ref[...], jnp.concatenate([high, low, high], 0))
            found = found + alternate * edge_columns[i : i + 1]
            inside = (jnp.abs(row_lag - row_offset[i : i + 1]) <= REACH) & (
                jnp.abs(col_lag - col_offset[i : i + 1]) <= REACH
            )
            weights = jnp.where(inside, jnp.exp(found * scale[i : i + 1]), 0.0)
            totals.append(jnp.sum(weights, axis=0, keepdims=True))
            row_totals.append(jnp.sum(weights * row_lag, axis=0, keepdims=True))
        out_ref[group] = exact(jnp.concatenate(totals, 0), gather_ref[0]) + exact(
            jnp.concatenate(row_totals, 0), gather_ref[1]
        )

    over_rows(0)

    def one(block, _):
        arrive(block)
        over_rows(block + 1)
        four_columns(2 * block)
        four_columns(2 * block + 1)
        return 0

    lax.fori_loop(0, blocks - 2, one, 0)
    over_rows(blocks - 1)
    four_columns(2 * (blocks - 2))


def plain_kernel(node_rows, *refs):
    match_core(node_rows, *refs, lambda block: None)


def pair_kernel(counts, node_rows, own_ref, *refs):
    (strips_ref, local_sem, send_sem, recv_sem, main_send, main_recv) = refs[-6:]
    slabs, columns, rows_of = counts
    z, x, y = lax.axis_index("gz"), lax.axis_index("gx"), lax.axis_index("gy")
    height, width = own_ref.shape
    main = node_rows * SPACING + MARGIN
    strip = main + MARGIN
    zero = jnp.bfloat16(0)
    strips_ref[:, :MARGIN, :] = jnp.full((2, MARGIN, width + 2 * BLOCK), zero)
    strips_ref[:, main:, :] = jnp.full((2, MARGIN, width + 2 * BLOCK), zero)
    strips_ref[:, :, :BLOCK] = jnp.full((2, strip, BLOCK), zero)
    strips_ref[:, :, BLOCK + width :] = jnp.full((2, strip, BLOCK), zero)

    def rows_at(start, size):
        return pl.ds(pl.multiple_of(start, MARGIN), size)

    def source_main(slab):
        return rows_at(slab * (height - main), main)

    def landed_main(slab):
        return rows_at((1 - slab) * MARGIN, main)

    def source_edge(slab):
        return rows_at((1 - slab) * (height - MARGIN), MARGIN)

    def landed_edge(slab):
        return rows_at(slab * main, MARGIN)

    left, right, centre = pl.ds(BLOCK - LANES, LANES), pl.ds(BLOCK + width, LANES), pl.ds(BLOCK, width)
    sides = (
        (1, pl.ds(width - LANES, LANES), left),
        (-1, pl.ds(0, LANES), right),
        (0, pl.ds(0, width), centre),
    )

    def inside(place, count):
        return (place >= 0) & (place < count)

    pieces = []
    for other in range(2):
        slab = z if other == 0 else 1 - z
        for vertical in range(2):
            for number, (shift, source_lanes, landed_lanes) in enumerate(sides):
                if shift == 0 and vertical == 0:
                    continue
                slot = (other * 2 + vertical) * 3 + number
                down = (1 - 2 * slab) * vertical
                source = (source_edge if vertical else source_main)(slab)
                landed = (landed_edge if vertical else landed_main)(slab)
                sent = pltpu.make_async_remote_copy(
                    src_ref=own_ref.at[source, source_lanes],
                    dst_ref=strips_ref.at[z, landed, landed_lanes],
                    send_sem=send_sem.at[slot],
                    recv_sem=recv_sem.at[slot],
                    device_id=(slab, x + shift, y + down),
                    device_id_type=MESH,
                )
                is_sent = inside(x + shift, columns) & inside(y + down, rows_of)
                mine = (landed_edge if vertical else landed_main)(z)
                up = (1 - 2 * z) * vertical
                giver = (slab, x - shift, y - up)
                comes = pltpu.make_async_remote_copy(
                    src_ref=own_ref.at[source, source_lanes],
                    dst_ref=strips_ref.at[slab, mine, landed_lanes],
                    send_sem=send_sem.at[slot],
                    recv_sem=recv_sem.at[slot],
                    device_id=giver,
                    device_id_type=MESH,
                )
                does_come = inside(x - shift, columns) & inside(y - up, rows_of)
                pieces.append((sent, is_sent, comes, does_come, giver))

    barrier = pltpu.get_barrier_semaphore()
    pl.semaphore_signal(barrier, inc=1, device_id=(1 - z, x, y), device_id_type=MESH)
    targets = jnp.int32(1)
    for _, is_sent, _, does_come, giver in pieces:

        @pl.when(does_come)
        def _():
            pl.semaphore_signal(barrier, inc=1, device_id=giver, device_id_type=MESH)

        targets = targets + is_sent.astype(jnp.int32)
    local = pltpu.make_async_copy(
        own_ref.at[source_main(z)], strips_ref.at[z, landed_main(z), centre], local_sem
    )
    local.start()
    pl.semaphore_wait(barrier, targets)

    for sent, is_sent, _, _, _ in pieces:
        pl.when(is_sent)(sent.start)

    def block_copy(block, section, slab):
        at = pl.multiple_of(block * BLOCK, BLOCK)
        return pltpu.make_async_remote_copy(
            src_ref=own_ref.at[source_main(1 - z), pl.ds(at, BLOCK)],
            dst_ref=strips_ref.at[section, landed_main(slab), pl.ds(BLOCK + at, BLOCK)],
            send_sem=main_send.at[block],
            recv_sem=main_recv.at[block],
            device_id=(1 - z, x, y),
            device_id_type=MESH,
        )

    blocks = width // BLOCK

    def start(block, _):
        block_copy(block, z, 1 - z).start()
        return 0

    lax.fori_loop(0, blocks, start, 0)
    local.wait()
    for _, _, comes, does_come, _ in pieces:
        pl.when(does_come)(comes.wait_recv)

    match_core(node_rows, strips_ref, *refs[:-6], lambda block: block_copy(block, 1 - z, z).wait_recv())

    def finish(block, _):
        block_copy(block, z, 1 - z).wait_send()
        return 0

    lax.fori_loop(0, blocks, finish, 0)
    for sent, is_sent, _, _, _ in pieces:
        pl.when(is_sent)(sent.wait_send)


def match(pixels, offsets, counts=None):
    node_rows, node_cols = offsets.shape[1:]
    groups = node_cols // 4 + 1
    width = node_cols * SPACING + 2 * BLOCK
    constants = [jnp.asarray(table) for table in tables()]
    shifted = jnp.pad(offsets.astype(jnp.float32), ((0, 0), (0, 0), (3, 1)))
    spread_offsets = jnp.repeat(shifted, PATCH, axis=2)
    scratch = [
        pltpu.VMEM((2, 2, node_rows * HALF, width), jnp.bfloat16),
        pltpu.VMEM((2, node_rows, width), jnp.float32),
        pltpu.VMEM((2, node_rows, width), jnp.float32),
    ]
    vmem = pl.BlockSpec(memory_space=pltpu.VMEM)
    specs = [vmem] * (2 + len(constants))
    if counts is None:
        body = functools.partial(plain_kernel, node_rows)
        params = pltpu.CompilerParams(vmem_limit_bytes=56 * 1024 * 1024)
    else:
        body = functools.partial(pair_kernel, counts, node_rows)
        params = pltpu.CompilerParams(
            vmem_limit_bytes=56 * 1024 * 1024, collective_id=0, has_side_effects=True
        )
        specs[0] = pl.BlockSpec(memory_space=pl.ANY)
        blocks = width // BLOCK - 2
        scratch += [
            pltpu.VMEM((2, (node_rows + 1) * SPACING, width), jnp.bfloat16),
            pltpu.SemaphoreType.DMA,
            pltpu.SemaphoreType.DMA((12,)),
            pltpu.SemaphoreType.DMA((12,)),
            pltpu.SemaphoreType.DMA((blocks,)),
            pltpu.SemaphoreType.DMA((blocks,)),
        ]
    out = pl.pallas_call(
        body,
        out_shape=jax.ShapeDtypeStruct((groups, node_rows, 128), jnp.float32),
        in_specs=specs,
        out_specs=vmem,
        scratch_shapes=scratch,
        compiler_params=params,
    )(pixels, spread_offsets, *constants)
    sums = jnp.transpose(out[:, :, :12].reshape(groups, node_rows, 3, 4), (2, 1, 0, 3))
    sums = sums.reshape(3, node_rows, 4 * groups)[:, :, 3:-1]
    return jnp.stack([sums[2] / sums[0], sums[1] / sums[0], sums[0]], 0)


def beside(value, axis, steps):
    count = lax.axis_size(axis)
    pairs = [(i, i + steps) for i in range(count) if 0 <= i + steps < count]
    return lax.ppermute(value, axis, pairs)


def bordered(field, axis, dim, width):
    length = field.shape[dim]
    before = beside(lax.slice_in_dim(field, length - width, length, axis=dim), axis, 1)
    after = beside(lax.slice_in_dim(field, 0, width, axis=dim), axis, -1)
    return before, after


def neighbour_sum(padded):
    return (
        padded[..., :-2, 1:-1]
        + padded[..., 2:, 1:-1]
        + padded[..., 1:-1, :-2]
        + padded[..., 1:-1, 2:]
    )


def relax(target, stiffness, living):
    fields = jnp.concatenate([target, stiffness[None], living[None]], 0)
    before, after = bordered(fields, "gx", 3, ITERS)
    fields = jnp.concatenate([before, fields, after], 3)
    before, after = bordered(fields, "gy", 2, ITERS)
    fields = jnp.concatenate([before, fields, after], 2)
    target, stiffness, living = fields[:2], fields[2], fields[3]
    moved = living[None] * target
    for _ in range(ITERS):
        pulled = neighbour_sum(living[None] * moved)
        count = neighbour_sum(living)
        inner = (slice(None), slice(1, -1), slice(1, -1))
        target, moved = target[(slice(None),) + inner], moved[(slice(None),) + inner]
        stiffness, living = stiffness[inner], living[inner]
        moved = (moved + stiffness[None] * target + living[None] * pulled) / (
            1.0 + stiffness + living * count
        )[None]
    return moved


def shards(section_pixels, tissue, peak_offsets):
    own = section_pixels[0]
    pixel_rows, pixel_cols = own.shape
    node_rows = pixel_rows // SPACING
    slabs = lax.axis_size("gz")
    place = lax.axis_index("gz")
    offsets = peak_offsets[:, 0].astype(jnp.float32)
    living = tissue.astype(jnp.float32)
    per_node = jnp.float32((2 * REACH + 1) ** 2)

    if slabs == 2 and node_rows % 16 == 0 and pixel_cols % BLOCK == 0:
        half_rows = node_rows // 2
        swap = [(0, 1), (1, 0)]
        first = place == 0
        nodes = jnp.concatenate([offsets, living], 0)
        other_nodes = lax.ppermute(nodes, "gz", swap)
        nodes_0 = jnp.where(first, nodes, other_nodes)
        nodes_1 = jnp.where(first, other_nodes, nodes)
        counts = tuple(lax.axis_size(axis) for axis in ("gz", "gx", "gy"))
        ours = match(
            own, lax.dynamic_slice_in_dim(nodes_0[:2], place * half_rows, half_rows, 1), counts
        )
        others = lax.ppermute(ours, "gz", swap)
        matched = jnp.concatenate(
            [jnp.where(first, ours, others), jnp.where(first, others, ours)], 1
        )
        target = jnp.stack([matched[:2], nodes_1[:2]], 1)
        alive = jnp.stack([nodes_0[2], nodes_1[2]], 0)
        stiffness = jnp.stack([nodes_0[2] * matched[2] / per_node, nodes_1[2]], 0)
        moved = relax(target, stiffness, alive)
        relaxed = jnp.where(first, moved[:, 0], moved[:, 1])
        placed = jnp.where(first, moved[:, 0], moved[:, 0] + moved[:, 1])
        return relaxed[:, None], placed[:, None]

    before, after = bordered(own, "gx", 1, LANES)
    own = jnp.concatenate([before, own, after], 1)
    before, after = bordered(own, "gy", 0, MARGIN)
    own = jnp.concatenate([before, own, after], 0)
    strips = jnp.pad(
        jnp.stack([own, beside(own, "gz", -1)], 0), ((0, 0), (0, 0), (BLOCK - LANES, BLOCK - LANES))
    )
    matched = match(strips, offsets)
    moved = relax(matched[:2, None], living * matched[2:] / per_node, living)
    placed = moved
    reach = 1
    while reach < slabs:
        placed = placed + beside(placed, "gz", reach)
        reach *= 2
    return moved, placed


def solution(mesh):
    placed = (P("gz", "gy", "gx"), P("gz", "gy", "gx"), P(None, "gz", "gy", "gx"))
    return jax.shard_map(
        shards,
        mesh=mesh,
        in_specs=placed,
        out_specs=(P(None, "gz", "gy", "gx"), P(None, "gz", "gy", "gx")),
        check_vma=False,
    )
```

```python
import functools
import math

import jax
import jax.numpy as jnp
import ml_dtypes
import numpy as np
from jax import lax
from jax.experimental import pallas as pl
from jax.experimental.pallas import tpu as pltpu
from jax.sharding import PartitionSpec as P

PATCH = 64
REACH = 12
SPACING = 32
ITERS = 3
BOUND = 8
FAR = BOUND + REACH
LAG_ROWS = 48
HALF = PATCH // 2
MARGIN = SPACING // 2
LANES = 128
BLOCK = 256
MESH = pl.DeviceIdType.MESH

sharpness = 32.0
tiny_energy = 1e-06


def bf16(table):
    return np.asarray(table, np.float32).astype(ml_dtypes.bfloat16)


def split(table):
    high = bf16(table)
    return high, bf16(np.asarray(table, np.float32) - high.astype(np.float32))


@functools.lru_cache(None)
def tables():
    n = np.arange(PATCH)
    angle = 2.0 * math.pi * ((n[:, None] * n[None, :]) % PATCH) / PATCH
    cosine, sine = np.cos(angle), np.sin(angle)
    row_table = np.zeros((80, PATCH))
    row_table[:HALF] = cosine[:HALF]
    row_table[HALF:PATCH] = -sine[:HALF]
    row_table[PATCH] = cosine[HALF]
    second = np.zeros((2, 256, 2, 2, 2, PATCH))
    spread = np.zeros((256, 4, PATCH))
    for pair in range(2):
        for q in range(2):
            node = 2 * pair + q
            rows = slice(MARGIN + SPACING * node, MARGIN + SPACING * node + PATCH)
            second[0, rows, pair, 0, q] = cosine.T
            second[0, rows, pair, 1, q] = -sine.T
            second[1, rows, pair, 0, q] = sine.T
            second[1, rows, pair, 1, q] = cosine.T
            spread[rows, node] = 1.0
    lags = np.arange(2 * FAR + 1) - FAR
    lag_angle = 2.0 * math.pi * ((n[:, None] * lags[None, :]) % PATCH) / PATCH
    lag_cos, lag_sin = np.cos(lag_angle), np.sin(lag_angle)
    back = np.zeros((2, 2, PATCH, 2, 2, PATCH))
    for q in range(2):
        back[0, q, :, 0, q, : lags.size] = lag_cos
        back[1, q, :, 0, q, : lags.size] = -lag_sin
        back[0, q, :, 1, q, : lags.size] = lag_sin
        back[1, q, :, 1, q, : lags.size] = lag_cos
    back_high, back_low = split(back.reshape(256, 256))
    fold = np.where(np.arange(HALF) == 0, 1.0, 2.0)[None]
    rows = np.zeros((LAG_ROWS, 2 * HALF))
    rows[: lags.size, :HALF] = fold * lag_cos[:HALF].T
    rows[: lags.size, HALF:] = -fold * lag_sin[:HALF].T
    row_high, row_low = split(rows)
    row_back = np.concatenate([row_high, row_high, row_low], 1)
    gather = np.zeros((2, 4, PATCH, 128))
    lane_lag = np.arange(PATCH) - FAR
    for node in range(4):
        gather[0, node, :, node] = 1.0
        gather[0, node, :, 4 + node] = lane_lag
        gather[1, node, :, 8 + node] = 1.0
    return (
        bf16(row_table),
        bf16(second.reshape(2, 256, 512)),
        np.asarray(spread.reshape(256, 256), np.float32),
        back_high,
        back_low,
        row_back,
        np.asarray(gather.reshape(2, 256, 128), np.float32),
    )


def match_core(
    node_rows,
    strips_ref,
    row_ref,
    second_ref,
    spread_ref,
    back_high_ref,
    back_low_ref,
    row_back_ref,
    gather_ref,
    half_ref,
    nyquist_ref,
    squares_ref,
    arrive,
    offsets_of,
    give,
):
    f32, b16 = jnp.float32, jnp.bfloat16
    blocks = strips_ref.shape[2] // BLOCK

    def dot(a, b):
        return jnp.dot(a, b, preferred_element_type=f32)

    def exact(a, b):
        return jnp.dot(a, b, preferred_element_type=f32, precision=lax.Precision.HIGHEST)

    def over_rows(block):
        lanes = pl.ds(pl.multiple_of(block * BLOCK, BLOCK), BLOCK)
        for which in range(2):
            for i in range(node_rows):
                rows = strips_ref[which, i * SPACING : i * SPACING + PATCH, lanes]
                got = dot(row_ref[...], rows)
                half_ref[which, 0, i * HALF : (i + 1) * HALF, lanes] = got[:HALF].astype(b16)
                half_ref[which, 1, i * HALF : (i + 1) * HALF, lanes] = got[HALF:PATCH].astype(b16)
                nyquist_ref[which, i : i + 1, lanes] = (
                    got[PATCH : PATCH + 1].astype(b16).astype(f32)
                )
                wide = rows.astype(f32)
                squares_ref[which, i : i + 1, lanes] = jnp.sum(wide * wide, axis=0, keepdims=True)

    row_lag = lax.broadcasted_iota(jnp.int32, (LAG_ROWS, BLOCK), 0) - FAR
    col_lag = (lax.broadcasted_iota(jnp.int32, (LAG_ROWS, BLOCK), 1) & (PATCH - 1)) - FAR
    alternate = jnp.where((row_lag & 1) == 0, 1.0, -1.0).astype(f32)
    row_lag = row_lag.astype(f32)
    col_lag = col_lag.astype(f32)

    def over_columns(first, then, pair):
        real, imag = slice(256 * pair, 256 * pair + 128), slice(256 * pair + 128, 256 * pair + 256)
        cross_real = first[:, real] * then[:, real] + first[:, imag] * then[:, imag]
        cross_imag = first[:, real] * then[:, imag] - first[:, imag] * then[:, real]
        cross = jnp.concatenate([cross_real, cross_imag], 1)
        high = cross.astype(b16)
        low = (cross - high.astype(f32)).astype(b16)
        return dot(high, back_high_ref[...]) + dot(low, back_high_ref[...]) + dot(high, back_low_ref[...])

    def four_columns(group):
        lanes = pl.ds(pl.multiple_of((group + 1) * LANES, LANES), BLOCK)
        spectra, edges, energies = [], [], []
        for which in range(2):
            spectra.append(
                dot(half_ref[which, 0, :, lanes], second_ref[0])
                + dot(half_ref[which, 1, :, lanes], second_ref[1])
            )
            edges.append(dot(nyquist_ref[which, :, lanes].astype(b16), second_ref[0]))
            energies.append(exact(squares_ref[which, :, lanes], spread_ref[...]))
        scale = (sharpness / (PATCH * PATCH)) / jnp.sqrt(energies[0] * energies[1] + tiny_energy)
        columns = [over_columns(spectra[0], spectra[1], pair) for pair in range(2)]
        edge_columns = jnp.concatenate(
            [over_columns(edges[0], edges[1], pair)[:, :128] for pair in range(2)], 1
        )
        row_offset, col_offset = offsets_of(group)
        totals, row_totals = [], []
        for i in range(node_rows):
            rows = slice(i * HALF, (i + 1) * HALF)
            field = jnp.concatenate(
                [
                    jnp.concatenate([columns[0][rows, :128], columns[1][rows, :128]], 1),
                    jnp.concatenate([columns[0][rows, 128:], columns[1][rows, 128:]], 1),
                ],
                0,
            )
            high = field.astype(b16)
            low = (field - high.astype(f32)).astype(b16)
            found = dot(row_back_ref[...], jnp.concatenate([high, low, high], 0))
            found = found + alternate * edge_columns[i : i + 1]
            inside = (jnp.abs(row_lag - row_offset[i : i + 1]) <= REACH) & (
                jnp.abs(col_lag - col_offset[i : i + 1]) <= REACH
            )
            weights = jnp.where(inside, jnp.exp(found * scale[i : i + 1]), 0.0)
            totals.append(jnp.sum(weights, axis=0, keepdims=True))
            row_totals.append(jnp.sum(weights * row_lag, axis=0, keepdims=True))
        sums = exact(jnp.concatenate(totals, 0), gather_ref[0])
        give(group, sums + exact(jnp.concatenate(row_totals, 0), gather_ref[1]))

    over_rows(0)

    def one(block, _):
        arrive(block)
        over_rows(block + 1)
        four_columns(2 * block)
        four_columns(2 * block + 1)
        return 0

    lax.fori_loop(0, blocks - 2, one, 0)
    over_rows(blocks - 1)
    four_columns(2 * (blocks - 2))


def plain_kernel(node_rows, strips_ref, offsets_ref, *refs):
    tables_of, (out_ref, *scratch) = refs[:7], refs[7:]

    def offsets_of(group):
        here = pl.ds(pl.multiple_of(group * BLOCK, BLOCK), BLOCK)
        return offsets_ref[0, :, here], offsets_ref[1, :, here]

    def give(group, sums):
        out_ref[group] = sums

    match_core(node_rows, strips_ref, *tables_of, *scratch, lambda block: None, offsets_of, give)


def pair_kernel(counts, node_rows, node_cols, own_ref, nodes_ref, four_ref, *refs):
    tables_of, (out_ref, *refs) = refs[:7], refs[7:]
    work, (
        strips_ref,
        sums_ref,
        ours_ref,
        nodes_in,
        found_in,
        local_sem,
        send_sem,
        recv_sem,
        main_send,
        main_recv,
        node_sem,
        node_send,
        node_recv,
        found_send,
        found_recv,
    ) = refs[:3], refs[3:]
    f32 = jnp.float32
    slabs, columns, rows_of = counts
    z, x, y = lax.axis_index("gz"), lax.axis_index("gx"), lax.axis_index("gy")
    height, width = own_ref.shape
    main = node_rows * SPACING + MARGIN
    strip = main + MARGIN
    zero = jnp.bfloat16(0)
    strips_ref[:, :MARGIN, :] = jnp.full((2, MARGIN, width + 2 * BLOCK), zero)
    strips_ref[:, main:, :] = jnp.full((2, MARGIN, width + 2 * BLOCK), zero)
    strips_ref[:, :, :BLOCK] = jnp.full((2, strip, BLOCK), zero)
    strips_ref[:, :, BLOCK + width :] = jnp.full((2, strip, BLOCK), zero)
    nodes_in[...] = jnp.zeros(nodes_in.shape, f32)
    found_in[...] = jnp.zeros(found_in.shape, f32)
    sums_ref[...] = jnp.zeros(sums_ref.shape, f32)

    def rows_at(start, size):
        return pl.ds(pl.multiple_of(start, MARGIN), size)

    def source_main(slab):
        return rows_at(slab * (height - main), main)

    def landed_main(slab):
        return rows_at((1 - slab) * MARGIN, main)

    def source_edge(slab):
        return rows_at((1 - slab) * (height - MARGIN), MARGIN)

    def landed_edge(slab):
        return rows_at(slab * main, MARGIN)

    left, right, centre = pl.ds(BLOCK - LANES, LANES), pl.ds(BLOCK + width, LANES), pl.ds(BLOCK, width)
    sides = (
        (1, pl.ds(width - LANES, LANES), left),
        (-1, pl.ds(0, LANES), right),
        (0, pl.ds(0, width), centre),
    )

    def inside(place, count):
        return (place >= 0) & (place < count)

    pieces = []
    for other in range(2):
        slab = z if other == 0 else 1 - z
        for vertical in range(2):
            for number, (shift, source_lanes, landed_lanes) in enumerate(sides):
                if shift == 0 and vertical == 0:
                    continue
                slot = (other * 2 + vertical) * 3 + number
                down = (1 - 2 * slab) * vertical
                source = (source_edge if vertical else source_main)(slab)
                landed = (landed_edge if vertical else landed_main)(slab)
                sent = pltpu.make_async_remote_copy(
                    src_ref=own_ref.at[source, source_lanes],
                    dst_ref=strips_ref.at[z, landed, landed_lanes],
                    send_sem=send_sem.at[slot],
                    recv_sem=recv_sem.at[slot],
                    device_id=(slab, x + shift, y + down),
                    device_id_type=MESH,
                )
                is_sent = inside(x + shift, columns) & inside(y + down, rows_of)
                mine = (landed_edge if vertical else landed_main)(z)
                up = (1 - 2 * z) * vertical
                giver = (slab, x - shift, y - up)
                comes = pltpu.make_async_remote_copy(
                    src_ref=own_ref.at[source, source_lanes],
                    dst_ref=strips_ref.at[slab, mine, landed_lanes],
                    send_sem=send_sem.at[slot],
                    recv_sem=recv_sem.at[slot],
                    device_id=giver,
                    device_id_type=MESH,
                )
                does_come = inside(x - shift, columns) & inside(y - up, rows_of)
                pieces.append((sent, is_sent, comes, does_come))

    def node_source(dy):
        if dy == 0:
            return pl.ds(0, 2 * node_rows)
        return pl.ds(node_rows if dy == 1 else 0, node_rows)

    def node_landed(dy):
        if dy == 0:
            return pl.ds(node_rows, 2 * node_rows)
        return pl.ds(0 if dy == 1 else 3 * node_rows, node_rows)

    around = [
        (other, dx, dy)
        for other in range(2)
        for dx in (-1, 0, 1)
        for dy in (-1, 0, 1)
        if (other, dx, dy) != (0, 0, 0)
    ]
    node_pieces = []
    for slot, (other, dx, dy) in enumerate(around):
        slab = z if other == 0 else 1 - z
        copies = []
        for section, device in ((z, (slab, x + dx, y + dy)), (slab, (slab, x - dx, y - dy))):
            copies.append(
                pltpu.make_async_remote_copy(
                    src_ref=nodes_ref.at[:, node_source(dy)],
                    dst_ref=nodes_in.at[section, 1 - dx, :, node_landed(dy)],
                    send_sem=node_send.at[slot],
                    recv_sem=node_recv.at[slot],
                    device_id=device,
                    device_id_type=MESH,
                )
            )
        goes = inside(x + dx, columns) & inside(y + dy, rows_of)
        comes = inside(x - dx, columns) & inside(y - dy, rows_of)
        node_pieces.append((copies[0], goes, copies[1], comes))

    found_pieces = []
    for other in range(2):
        for dx in (-1, 0, 1):
            for vertical in range(2):
                if (other, dx, vertical) == (0, 0, 0):
                    continue
                slot = (other * 3 + dx + 1) * 2 + vertical
                slab = z if other == 0 else 1 - z
                copies = []
                for finder, sign in ((z, 1), (slab, -1)):
                    down = (2 * finder - 1) * vertical
                    row = (1 + finder) * node_rows if vertical == 0 else 3 * (1 - finder) * node_rows
                    copies.append(
                        (
                            pltpu.make_async_remote_copy(
                                src_ref=ours_ref,
                                dst_ref=found_in.at[
                                    1 - dx, :, pl.ds(pl.multiple_of(row, node_rows), node_rows)
                                ],
                                send_sem=found_send.at[slot],
                                recv_sem=found_recv.at[slot],
                                device_id=(slab, x + sign * dx, y + sign * down),
                                device_id_type=MESH,
                            ),
                            inside(x + sign * dx, columns) & inside(y + sign * down, rows_of),
                        )
                    )
                found_pieces.append(copies[0] + copies[1])

    barrier = pltpu.get_barrier_semaphore()
    targets = jnp.int32(0)
    for other, dx, dy in around:
        there = inside(x + dx, columns) & inside(y + dy, rows_of)

        @pl.when(there)
        def _():
            pl.semaphore_signal(
                barrier,
                inc=1,
                device_id=(z if other == 0 else 1 - z, x + dx, y + dy),
                device_id_type=MESH,
            )

        targets = targets + there.astype(jnp.int32)
    own_nodes = pltpu.make_async_copy(
        nodes_ref, nodes_in.at[z, 1, :, node_landed(0)], node_sem
    )
    own_nodes.start()
    local = pltpu.make_async_copy(
        own_ref.at[source_main(z)], strips_ref.at[z, landed_main(z), centre], local_sem
    )
    local.start()
    pl.semaphore_wait(barrier, targets)

    for sent, is_sent, _, _ in pieces + node_pieces:
        pl.when(is_sent)(sent.start)

    def block_copy(block, section, slab):
        at = pl.multiple_of(block * BLOCK, BLOCK)
        return pltpu.make_async_remote_copy(
            src_ref=own_ref.at[source_main(1 - z), pl.ds(at, BLOCK)],
            dst_ref=strips_ref.at[section, landed_main(slab), pl.ds(BLOCK + at, BLOCK)],
            send_sem=main_send.at[block],
            recv_sem=main_recv.at[block],
            device_id=(1 - z, x, y),
            device_id_type=MESH,
        )

    blocks = width // BLOCK

    def start(block, _):
        block_copy(block, z, 1 - z).start()
        return 0

    lax.fori_loop(0, blocks, start, 0)
    local.wait()
    own_nodes.wait()
    for _, _, comes, does_come in pieces + node_pieces:
        pl.when(does_come)(comes.wait_recv)

    upper = pl.ds(pl.multiple_of((1 + z) * node_rows, node_rows), node_rows)

    def offsets_of(group):
        return [
            jnp.dot(
                pltpu.roll(nodes_in[0, 1, part, upper, :], lax.rem(LANES - 4 * group, LANES), 1).astype(
                    jnp.bfloat16
                ),
                four_ref[...],
                preferred_element_type=f32,
            )
            for part in range(2)
        ]

    few = lax.broadcasted_iota(jnp.int32, (node_rows, LANES), 1)

    def give(group, sums):
        for part in range(3):
            one = jnp.where((few >= 4 * part) & (few < 4 * part + 4), sums, 0.0)
            sums_ref[part] += pltpu.roll(one, lax.rem(4 * group - 4 * part + LANES, LANES), 1)

    match_core(
        node_rows,
        strips_ref,
        *tables_of,
        *work,
        lambda block: block_copy(block, 1 - z, z).wait_recv(),
        offsets_of,
        give,
    )
    total = sums_ref[0]
    held = (few >= ITERS) & (few < ITERS + node_cols)
    ours_ref[0] = jnp.where(held, sums_ref[2] / total, 0.0)
    ours_ref[1] = jnp.where(held, sums_ref[1] / total, 0.0)
    ours_ref[2] = jnp.where(held, total, 0.0)
    for sent, is_sent, _, _ in found_pieces:
        pl.when(is_sent)(sent.start)
    found_in[1, :, upper, :] = ours_ref[...]

    lane = lax.broadcasted_iota(jnp.int32, (4 * node_rows, LANES), 1)

    def joined(ref, at):
        before = pltpu.roll(ref[at(0)], LANES - node_cols, 1)
        after = pltpu.roll(ref[at(2)], node_cols, 1)
        value = jnp.where(lane < ITERS, before, ref[at(1)])
        value = jnp.where(lane < ITERS + node_cols, value, after)
        return jnp.where(lane < 2 * ITERS + node_cols, value, 0.0)

    nodes = [[joined(nodes_in, lambda k: (s, k, part)) for part in range(3)] for s in range(2)]
    for _, _, comes, does_come in found_pieces:
        pl.when(does_come)(comes.wait_recv)
    found = [joined(found_in, lambda k: (k, part)) for part in range(3)]

    def neighbours(value):
        rows = 4 * node_rows
        return (
            pltpu.roll(value, 1, 0)
            + pltpu.roll(value, rows - 1, 0)
            + pltpu.roll(value, 1, 1)
            + pltpu.roll(value, LANES - 1, 1)
        )

    per_node = float((2 * REACH + 1) ** 2)
    moved = []
    for section in range(2):
        living = nodes[section][2]
        targets = found[:2] if section == 0 else nodes[1][:2]
        stiffness = living * found[2] / per_node if section == 0 else living
        below = 1.0 + stiffness + living * neighbours(living)
        for part in range(2):
            value = living * targets[part]
            for _ in range(ITERS):
                value = (
                    value + stiffness * targets[part] + living * neighbours(living * value)
                ) / below
            moved.append(value[node_rows : 3 * node_rows])
    first = z == 0
    for part in range(2):
        out_ref[0, part] = jnp.where(first, moved[part], moved[2 + part])
        out_ref[1, part] = jnp.where(first, moved[part], moved[part] + moved[2 + part])

    def finish(block, _):
        block_copy(block, z, 1 - z).wait_send()
        return 0

    lax.fori_loop(0, blocks, finish, 0)
    for sent, is_sent, _, _ in pieces + node_pieces + found_pieces:
        pl.when(is_sent)(sent.wait_send)


def working_scratch(node_rows, width):
    return [
        pltpu.VMEM((2, 2, node_rows * HALF, width), jnp.bfloat16),
        pltpu.VMEM((2, node_rows, width), jnp.float32),
        pltpu.VMEM((2, node_rows, width), jnp.float32),
    ]


def match_pair(own, nodes, counts):
    node_cols = nodes.shape[2]
    node_rows = nodes.shape[1] // 2
    width = own.shape[1] + 2 * BLOCK
    blocks = width // BLOCK - 2
    four = np.zeros((LANES, 4, PATCH))
    for node in range(4):
        four[node, node] = 1.0
    constants = [jnp.asarray(t) for t in (bf16(four.reshape(LANES, BLOCK)),) + tables()]
    laid = jnp.pad(nodes, ((0, 0), (0, 0), (ITERS, LANES - ITERS - node_cols)))
    vmem = pl.BlockSpec(memory_space=pltpu.VMEM)
    dma = pltpu.SemaphoreType.DMA
    f32 = jnp.float32
    out = pl.pallas_call(
        functools.partial(pair_kernel, counts, node_rows, node_cols),
        out_shape=jax.ShapeDtypeStruct((2, 2, 2 * node_rows, LANES), f32),
        in_specs=[pl.BlockSpec(memory_space=pl.ANY)] + [vmem] * (1 + len(constants)),
        out_specs=vmem,
        scratch_shapes=working_scratch(node_rows, width)
        + [
            pltpu.VMEM((2, (node_rows + 1) * SPACING, width), jnp.bfloat16),
            pltpu.VMEM((3, node_rows, LANES), f32),
            pltpu.VMEM((3, node_rows, LANES), f32),
            pltpu.VMEM((2, 3, 3, 4 * node_rows, LANES), f32),
            pltpu.VMEM((3, 3, 4 * node_rows, LANES), f32),
            dma,
            dma((12,)),
            dma((12,)),
            dma((blocks,)),
            dma((blocks,)),
            dma,
            dma((17,)),
            dma((17,)),
            dma((12,)),
            dma((12,)),
        ],
        compiler_params=pltpu.CompilerParams(
            vmem_limit_bytes=56 * 1024 * 1024, collective_id=0, has_side_effects=True
        ),
    )(own, laid, *constants)
    out = out[..., ITERS : ITERS + node_cols]
    return out[0], out[1]


def match(strips, offsets):
    node_rows, node_cols = offsets.shape[1:]
    groups = node_cols // 4 + 1
    constants = [jnp.asarray(table) for table in tables()]
    shifted = jnp.pad(offsets.astype(jnp.float32), ((0, 0), (0, 0), (3, 1)))
    spread_offsets = jnp.repeat(shifted, PATCH, axis=2)
    vmem = pl.BlockSpec(memory_space=pltpu.VMEM)
    out = pl.pallas_call(
        functools.partial(plain_kernel, node_rows),
        out_shape=jax.ShapeDtypeStruct((groups, node_rows, 128), jnp.float32),
        in_specs=[vmem] * (2 + len(constants)),
        out_specs=vmem,
        scratch_shapes=working_scratch(node_rows, strips.shape[2]),
        compiler_params=pltpu.CompilerParams(vmem_limit_bytes=56 * 1024 * 1024),
    )(strips, spread_offsets, *constants)
    sums = jnp.transpose(out[:, :, :12].reshape(groups, node_rows, 3, 4), (2, 1, 0, 3))
    sums = sums.reshape(3, node_rows, 4 * groups)[:, :, 3:-1]
    return jnp.stack([sums[2] / sums[0], sums[1] / sums[0], sums[0]], 0)


def beside(value, axis, steps):
    count = lax.axis_size(axis)
    pairs = [(i, i + steps) for i in range(count) if 0 <= i + steps < count]
    return lax.ppermute(value, axis, pairs)


def bordered(field, axis, dim, width):
    length = field.shape[dim]
    before = beside(lax.slice_in_dim(field, length - width, length, axis=dim), axis, 1)
    after = beside(lax.slice_in_dim(field, 0, width, axis=dim), axis, -1)
    return before, after


def neighbour_sum(padded):
    return (
        padded[..., :-2, 1:-1]
        + padded[..., 2:, 1:-1]
        + padded[..., 1:-1, :-2]
        + padded[..., 1:-1, 2:]
    )


def relax(target, stiffness, living):
    fields = jnp.concatenate([target, stiffness[None], living[None]], 0)
    before, after = bordered(fields, "gx", 3, ITERS)
    fields = jnp.concatenate([before, fields, after], 3)
    before, after = bordered(fields, "gy", 2, ITERS)
    fields = jnp.concatenate([before, fields, after], 2)
    target, stiffness, living = fields[:2], fields[2], fields[3]
    moved = living[None] * target
    for _ in range(ITERS):
        pulled = neighbour_sum(living[None] * moved)
        count = neighbour_sum(living)
        inner = (slice(None), slice(1, -1), slice(1, -1))
        target, moved = target[(slice(None),) + inner], moved[(slice(None),) + inner]
        stiffness, living = stiffness[inner], living[inner]
        moved = (moved + stiffness[None] * target + living[None] * pulled) / (
            1.0 + stiffness + living * count
        )[None]
    return moved


def shards(section_pixels, tissue, peak_offsets):
    own = section_pixels[0]
    pixel_rows, pixel_cols = own.shape
    node_rows = pixel_rows // SPACING
    slabs = lax.axis_size("gz")
    offsets = peak_offsets[:, 0].astype(jnp.float32)
    living = tissue.astype(jnp.float32)
    per_node = jnp.float32((2 * REACH + 1) ** 2)

    if (
        slabs == 2
        and node_rows % 16 == 0
        and pixel_cols % BLOCK == 0
        and pixel_cols // SPACING + 2 * ITERS <= LANES
    ):
        counts = tuple(lax.axis_size(axis) for axis in ("gz", "gx", "gy"))
        moved, placed = match_pair(own, jnp.concatenate([offsets, living], 0), counts)
        return moved[:, None], placed[:, None]

    before, after = bordered(own, "gx", 1, LANES)
    own = jnp.concatenate([before, own, after], 1)
    before, after = bordered(own, "gy", 0, MARGIN)
    own = jnp.concatenate([before, own, after], 0)
    strips = jnp.pad(
        jnp.stack([own, beside(own, "gz", -1)], 0), ((0, 0), (0, 0), (BLOCK - LANES, BLOCK - LANES))
    )
    matched = match(strips, offsets)
    moved = relax(matched[:2, None], living * matched[2:] / per_node, living)
    placed = moved
    reach = 1
    while reach < slabs:
        placed = placed + beside(placed, "gz", reach)
        reach *= 2
    return moved, placed


def solution(mesh):
    placed = (P("gz", "gy", "gx"), P("gz", "gy", "gx"), P(None, "gz", "gy", "gx"))
    return jax.shard_map(
        shards,
        mesh=mesh,
        in_specs=placed,
        out_specs=(P(None, "gz", "gy", "gx"), P(None, "gz", "gy", "gx")),
        check_vma=False,
    )
```

```python
import functools
import math

import jax
import jax.numpy as jnp
import ml_dtypes
import numpy as np
from jax import lax
from jax.experimental import pallas as pl
from jax.experimental.pallas import tpu as pltpu
from jax.sharding import PartitionSpec as P

PATCH = 64
REACH = 12
SPACING = 32
ITERS = 3
BOUND = 8
FAR = BOUND + REACH
LAG_ROWS = 48
HALF = PATCH // 2
MARGIN = SPACING // 2
LANES = 128
BLOCK = 256
MESH = pl.DeviceIdType.MESH

sharpness = 32.0
tiny_energy = 1e-06


def bf16(table):
    return np.asarray(table, np.float32).astype(ml_dtypes.bfloat16)


def split(table):
    high = bf16(table)
    return high, bf16(np.asarray(table, np.float32) - high.astype(np.float32))


@functools.lru_cache(None)
def tables():
    n = np.arange(PATCH)
    angle = 2.0 * math.pi * ((n[:, None] * n[None, :]) % PATCH) / PATCH
    cosine, sine = np.cos(angle), np.sin(angle)
    row_table = np.zeros((80, PATCH))
    row_table[:HALF] = cosine[:HALF]
    row_table[HALF:PATCH] = -sine[:HALF]
    row_table[PATCH] = cosine[HALF]
    second = np.zeros((2, 256, 2, 2, 2, PATCH))
    spread = np.zeros((256, 4, PATCH))
    for pair in range(2):
        for q in range(2):
            node = 2 * pair + q
            rows = slice(MARGIN + SPACING * node, MARGIN + SPACING * node + PATCH)
            second[0, rows, pair, 0, q] = cosine.T
            second[0, rows, pair, 1, q] = -sine.T
            second[1, rows, pair, 0, q] = sine.T
            second[1, rows, pair, 1, q] = cosine.T
            spread[rows, node] = 1.0
    lags = np.arange(2 * FAR + 1) - FAR
    lag_angle = 2.0 * math.pi * ((n[:, None] * lags[None, :]) % PATCH) / PATCH
    lag_cos, lag_sin = np.cos(lag_angle), np.sin(lag_angle)
    back = np.zeros((2, 2, PATCH, 2, 2, PATCH))
    for q in range(2):
        back[0, q, :, 0, q, : lags.size] = lag_cos
        back[1, q, :, 0, q, : lags.size] = -lag_sin
        back[0, q, :, 1, q, : lags.size] = lag_sin
        back[1, q, :, 1, q, : lags.size] = lag_cos
    back_high, back_low = split(back.reshape(256, 256))
    fold = np.where(np.arange(HALF) == 0, 1.0, 2.0)[None]
    rows = np.zeros((LAG_ROWS, 2 * HALF))
    rows[: lags.size, :HALF] = fold * lag_cos[:HALF].T
    rows[: lags.size, HALF:] = -fold * lag_sin[:HALF].T
    row_high, row_low = split(rows)
    row_back = np.concatenate([row_high, row_high, row_low], 1)
    gather = np.zeros((4, PATCH, 128))
    lane_lag = np.arange(PATCH) - FAR
    for node in range(4):
        gather[node, :, node] = 1.0
        gather[node, :, 4 + node] = lane_lag
    return (
        bf16(row_table),
        bf16(second.reshape(2, 256, 512)),
        bf16(spread.reshape(256, 256)),
        back_high,
        back_low,
        row_back,
        bf16(gather.reshape(256, 128)),
    )


def match_core(
    node_rows,
    strips_ref,
    row_ref,
    second_ref,
    spread_ref,
    back_high_ref,
    back_low_ref,
    row_back_ref,
    gather_ref,
    half_ref,
    nyquist_ref,
    squares_ref,
    arrive,
    offsets_of,
    give,
):
    f32, b16 = jnp.float32, jnp.bfloat16
    blocks = strips_ref.shape[2] // BLOCK

    def dot(a, b):
        return jnp.dot(a, b, preferred_element_type=f32)

    def parts(value):
        high = value.astype(b16)
        rest = value - high.astype(f32)
        middle = rest.astype(b16)
        return [high.astype(f32), middle.astype(f32), rest - middle.astype(f32)]

    def exact_pair(first, then, table):
        stacked = jnp.concatenate(parts(first) + parts(then), 0).astype(b16)
        got = dot(stacked, table)
        n = first.shape[0]
        terms = [got[k * n : (k + 1) * n] for k in range(6)]
        return terms[0] + terms[1] + terms[2], terms[3] + terms[4] + terms[5]

    def over_rows(block):
        lanes = pl.ds(pl.multiple_of(block * BLOCK, BLOCK), BLOCK)
        for which in range(2):
            for i in range(node_rows):
                rows = strips_ref[which, i * SPACING : i * SPACING + PATCH, lanes]
                got = dot(row_ref[...], rows)
                half_ref[which, 0, i * HALF : (i + 1) * HALF, lanes] = got[:HALF].astype(b16)
                half_ref[which, 1, i * HALF : (i + 1) * HALF, lanes] = got[HALF:PATCH].astype(b16)
                nyquist_ref[which, i : i + 1, lanes] = (
                    got[PATCH : PATCH + 1].astype(b16).astype(f32)
                )
                wide = rows.astype(f32)
                squares_ref[which, i : i + 1, lanes] = jnp.sum(wide * wide, axis=0, keepdims=True)

    row_lag = lax.broadcasted_iota(jnp.int32, (LAG_ROWS, BLOCK), 0) - FAR
    col_lag = (lax.broadcasted_iota(jnp.int32, (LAG_ROWS, BLOCK), 1) & (PATCH - 1)) - FAR
    alternate = jnp.where((row_lag & 1) == 0, 1.0, -1.0).astype(f32)
    row_lag = row_lag.astype(f32)
    col_lag = col_lag.astype(f32)

    def crossed(first, then, pair):
        real, imag = slice(256 * pair, 256 * pair + 128), slice(256 * pair + 128, 256 * pair + 256)
        cross_real = first[:, real] * then[:, real] + first[:, imag] * then[:, imag]
        cross_imag = first[:, real] * then[:, imag] - first[:, imag] * then[:, real]
        return jnp.concatenate([cross_real, cross_imag], 1)

    def over_columns(cross):
        high = cross.astype(b16)
        low = (cross - high.astype(f32)).astype(b16)
        return dot(high, back_high_ref[...]) + dot(low, back_high_ref[...]) + dot(high, back_low_ref[...])

    def four_columns(group):
        lanes = pl.ds(pl.multiple_of((group + 1) * LANES, LANES), BLOCK)
        spectra = []
        for which in range(2):
            spectra.append(
                dot(half_ref[which, 0, :, lanes], second_ref[0])
                + dot(half_ref[which, 1, :, lanes], second_ref[1])
            )
        both = jnp.concatenate([nyquist_ref[0, :, lanes], nyquist_ref[1, :, lanes]], 0)
        edges = dot(both.astype(b16), second_ref[0])
        energies = exact_pair(squares_ref[0, :, lanes], squares_ref[1, :, lanes], spread_ref[...])
        scale = (sharpness / (PATCH * PATCH)) / jnp.sqrt(energies[0] * energies[1] + tiny_energy)
        main = node_rows * HALF
        back = over_columns(
            jnp.concatenate(
                [crossed(spectra[0], spectra[1], pair) for pair in range(2)]
                + [crossed(edges[:node_rows], edges[node_rows:], pair) for pair in range(2)],
                0,
            )
        )
        columns = [back[:main], back[main : 2 * main]]
        edge_columns = jnp.concatenate(
            [back[2 * main : 2 * main + node_rows, :128], back[2 * main + node_rows :, :128]], 1
        )
        row_offset, col_offset = offsets_of(group)
        totals, row_totals = [], []
        for i in range(node_rows):
            rows = slice(i * HALF, (i + 1) * HALF)
            field = jnp.concatenate(
                [
                    jnp.concatenate([columns[0][rows, :128], columns[1][rows, :128]], 1),
                    jnp.concatenate([columns[0][rows, 128:], columns[1][rows, 128:]], 1),
                ],
                0,
            )
            high = field.astype(b16)
            low = (field - high.astype(f32)).astype(b16)
            found = dot(row_back_ref[...], jnp.concatenate([high, low, high], 0))
            found = found + alternate * edge_columns[i : i + 1]
            inside = (jnp.abs(row_lag - row_offset[i : i + 1]) <= REACH) & (
                jnp.abs(col_lag - col_offset[i : i + 1]) <= REACH
            )
            weights = jnp.where(inside, jnp.exp(found * scale[i : i + 1]), 0.0)
            totals.append(jnp.sum(weights, axis=0, keepdims=True))
            row_totals.append(jnp.sum(weights * row_lag, axis=0, keepdims=True))
        plain, by_row = exact_pair(
            jnp.concatenate(totals, 0), jnp.concatenate(row_totals, 0), gather_ref[...]
        )
        few = lax.broadcasted_iota(jnp.int32, (node_rows, LANES), 1)
        give(group, plain + pltpu.roll(jnp.where(few < 4, by_row, 0.0), 8, 1))

    over_rows(0)

    def one(block, _):
        arrive(block)
        over_rows(block + 1)
        four_columns(2 * block)
        four_columns(2 * block + 1)
        return 0

    lax.fori_loop(0, blocks - 2, one, 0)
    over_rows(blocks - 1)
    four_columns(2 * (blocks - 2))


def plain_kernel(node_rows, strips_ref, offsets_ref, *refs):
    tables_of, (out_ref, *scratch) = refs[:7], refs[7:]

    def offsets_of(group):
        here = pl.ds(pl.multiple_of(group * BLOCK, BLOCK), BLOCK)
        return offsets_ref[0, :, here], offsets_ref[1, :, here]

    def give(group, sums):
        out_ref[group] = sums

    match_core(node_rows, strips_ref, *tables_of, *scratch, lambda block: None, offsets_of, give)


def pair_kernel(counts, node_rows, node_cols, own_ref, nodes_ref, four_ref, *refs):
    tables_of, (out_ref, *refs) = refs[:7], refs[7:]
    work, (
        strips_ref,
        sums_ref,
        ours_ref,
        nodes_in,
        found_in,
        local_sem,
        send_sem,
        recv_sem,
        main_send,
        main_recv,
        node_sem,
        node_send,
        node_recv,
        found_send,
        found_recv,
    ) = refs[:3], refs[3:]
    f32 = jnp.float32
    slabs, columns, rows_of = counts
    z, x, y = lax.axis_index("gz"), lax.axis_index("gx"), lax.axis_index("gy")
    height, width = own_ref.shape
    main = node_rows * SPACING + MARGIN
    strip = main + MARGIN
    zero = jnp.bfloat16(0)
    strips_ref[:, :MARGIN, :] = jnp.full((2, MARGIN, width + 2 * BLOCK), zero)
    strips_ref[:, main:, :] = jnp.full((2, MARGIN, width + 2 * BLOCK), zero)
    strips_ref[:, :, :BLOCK] = jnp.full((2, strip, BLOCK), zero)
    strips_ref[:, :, BLOCK + width :] = jnp.full((2, strip, BLOCK), zero)
    nodes_in[...] = jnp.zeros(nodes_in.shape, f32)
    found_in[...] = jnp.zeros(found_in.shape, f32)
    sums_ref[...] = jnp.zeros(sums_ref.shape, f32)

    def rows_at(start, size):
        return pl.ds(pl.multiple_of(start, MARGIN), size)

    def source_main(slab):
        return rows_at(slab * (height - main), main)

    def landed_main(slab):
        return rows_at((1 - slab) * MARGIN, main)

    def source_edge(slab):
        return rows_at((1 - slab) * (height - MARGIN), MARGIN)

    def landed_edge(slab):
        return rows_at(slab * main, MARGIN)

    left, right, centre = pl.ds(BLOCK - LANES, LANES), pl.ds(BLOCK + width, LANES), pl.ds(BLOCK, width)
    sides = (
        (1, pl.ds(width - LANES, LANES), left),
        (-1, pl.ds(0, LANES), right),
        (0, pl.ds(0, width), centre),
    )

    def inside(place, count):
        return (place >= 0) & (place < count)

    pieces = []
    for other in range(2):
        slab = z if other == 0 else 1 - z
        for vertical in range(2):
            for number, (shift, source_lanes, landed_lanes) in enumerate(sides):
                if shift == 0 and vertical == 0:
                    continue
                slot = (other * 2 + vertical) * 3 + number
                down = (1 - 2 * slab) * vertical
                source = (source_edge if vertical else source_main)(slab)
                landed = (landed_edge if vertical else landed_main)(slab)
                sent = pltpu.make_async_remote_copy(
                    src_ref=own_ref.at[source, source_lanes],
                    dst_ref=strips_ref.at[z, landed, landed_lanes],
                    send_sem=send_sem.at[slot],
                    recv_sem=recv_sem.at[slot],
                    device_id=(slab, x + shift, y + down),
                    device_id_type=MESH,
                )
                is_sent = inside(x + shift, columns) & inside(y + down, rows_of)
                mine = (landed_edge if vertical else landed_main)(z)
                up = (1 - 2 * z) * vertical
                giver = (slab, x - shift, y - up)
                comes = pltpu.make_async_remote_copy(
                    src_ref=own_ref.at[source, source_lanes],
                    dst_ref=strips_ref.at[slab, mine, landed_lanes],
                    send_sem=send_sem.at[slot],
                    recv_sem=recv_sem.at[slot],
                    device_id=giver,
                    device_id_type=MESH,
                )
                does_come = inside(x - shift, columns) & inside(y - up, rows_of)
                pieces.append((sent, is_sent, comes, does_come))

    def node_source(dy):
        if dy == 0:
            return pl.ds(0, 2 * node_rows)
        return pl.ds(node_rows if dy == 1 else 0, node_rows)

    def node_landed(dy):
        if dy == 0:
            return pl.ds(node_rows, 2 * node_rows)
        return pl.ds(0 if dy == 1 else 3 * node_rows, node_rows)

    around = [
        (other, dx, dy)
        for other in range(2)
        for dx in (-1, 0, 1)
        for dy in (-1, 0, 1)
        if (other, dx, dy) != (0, 0, 0)
    ]
    node_pieces = []
    for slot, (other, dx, dy) in enumerate(around):
        slab = z if other == 0 else 1 - z
        copies = []
        for section, device in ((z, (slab, x + dx, y + dy)), (slab, (slab, x - dx, y - dy))):
            copies.append(
                pltpu.make_async_remote_copy(
                    src_ref=nodes_ref.at[:, node_source(dy)],
                    dst_ref=nodes_in.at[section, 1 - dx, :, node_landed(dy)],
                    send_sem=node_send.at[slot],
                    recv_sem=node_recv.at[slot],
                    device_id=device,
                    device_id_type=MESH,
                )
            )
        goes = inside(x + dx, columns) & inside(y + dy, rows_of)
        comes = inside(x - dx, columns) & inside(y - dy, rows_of)
        node_pieces.append((copies[0], goes, copies[1], comes))

    found_pieces = []
    for other in range(2):
        for dx in (-1, 0, 1):
            for vertical in range(2):
                if (other, dx, vertical) == (0, 0, 0):
                    continue
                slot = (other * 3 + dx + 1) * 2 + vertical
                slab = z if other == 0 else 1 - z
                copies = []
                for finder, sign in ((z, 1), (slab, -1)):
                    down = (2 * finder - 1) * vertical
                    row = (1 + finder) * node_rows if vertical == 0 else 3 * (1 - finder) * node_rows
                    copies.append(
                        (
                            pltpu.make_async_remote_copy(
                                src_ref=ours_ref,
                                dst_ref=found_in.at[
                                    1 - dx, :, pl.ds(pl.multiple_of(row, node_rows), node_rows)
                                ],
                                send_sem=found_send.at[slot],
                                recv_sem=found_recv.at[slot],
                                device_id=(slab, x + sign * dx, y + sign * down),
                                device_id_type=MESH,
                            ),
                            inside(x + sign * dx, columns) & inside(y + sign * down, rows_of),
                        )
                    )
                found_pieces.append(copies[0] + copies[1])

    barrier = pltpu.get_barrier_semaphore()
    targets = jnp.int32(0)
    for other, dx, dy in around:
        there = inside(x + dx, columns) & inside(y + dy, rows_of)

        @pl.when(there)
        def _():
            pl.semaphore_signal(
                barrier,
                inc=1,
                device_id=(z if other == 0 else 1 - z, x + dx, y + dy),
                device_id_type=MESH,
            )

        targets = targets + there.astype(jnp.int32)
    own_nodes = pltpu.make_async_copy(
        nodes_ref, nodes_in.at[z, 1, :, node_landed(0)], node_sem
    )
    own_nodes.start()
    local = pltpu.make_async_copy(
        own_ref.at[source_main(z)], strips_ref.at[z, landed_main(z), centre], local_sem
    )
    local.start()
    pl.semaphore_wait(barrier, targets)

    for sent, is_sent, _, _ in pieces + node_pieces:
        pl.when(is_sent)(sent.start)

    def block_copy(block, section, slab):
        at = pl.multiple_of(block * BLOCK, BLOCK)
        return pltpu.make_async_remote_copy(
            src_ref=own_ref.at[source_main(1 - z), pl.ds(at, BLOCK)],
            dst_ref=strips_ref.at[section, landed_main(slab), pl.ds(BLOCK + at, BLOCK)],
            send_sem=main_send.at[block],
            recv_sem=main_recv.at[block],
            device_id=(1 - z, x, y),
            device_id_type=MESH,
        )

    blocks = width // BLOCK

    def start(block, _):
        block_copy(block, z, 1 - z).start()
        return 0

    lax.fori_loop(0, blocks, start, 0)
    local.wait()
    own_nodes.wait()
    for _, _, comes, does_come in pieces + node_pieces:
        pl.when(does_come)(comes.wait_recv)

    upper = pl.ds(pl.multiple_of((1 + z) * node_rows, node_rows), node_rows)

    def offsets_of(group):
        return [
            jnp.dot(
                pltpu.roll(nodes_in[0, 1, part, upper, :], lax.rem(LANES - 4 * group, LANES), 1).astype(
                    jnp.bfloat16
                ),
                four_ref[...],
                preferred_element_type=f32,
            )
            for part in range(2)
        ]

    few = lax.broadcasted_iota(jnp.int32, (node_rows, LANES), 1)

    def give(group, sums):
        for part in range(3):
            one = jnp.where((few >= 4 * part) & (few < 4 * part + 4), sums, 0.0)
            sums_ref[part] += pltpu.roll(one, lax.rem(4 * group - 4 * part + LANES, LANES), 1)

    match_core(
        node_rows,
        strips_ref,
        *tables_of,
        *work,
        lambda block: block_copy(block, 1 - z, z).wait_recv(),
        offsets_of,
        give,
    )
    total = sums_ref[0]
    held = (few >= ITERS) & (few < ITERS + node_cols)
    ours_ref[0] = jnp.where(held, sums_ref[2] / total, 0.0)
    ours_ref[1] = jnp.where(held, sums_ref[1] / total, 0.0)
    ours_ref[2] = jnp.where(held, total, 0.0)
    for sent, is_sent, _, _ in found_pieces:
        pl.when(is_sent)(sent.start)
    found_in[1, :, upper, :] = ours_ref[...]

    lane = lax.broadcasted_iota(jnp.int32, (4 * node_rows, LANES), 1)

    def joined(ref, at):
        before = pltpu.roll(ref[at(0)], LANES - node_cols, 1)
        after = pltpu.roll(ref[at(2)], node_cols, 1)
        value = jnp.where(lane < ITERS, before, ref[at(1)])
        value = jnp.where(lane < ITERS + node_cols, value, after)
        return jnp.where(lane < 2 * ITERS + node_cols, value, 0.0)

    nodes = [[joined(nodes_in, lambda k: (s, k, part)) for part in range(3)] for s in range(2)]
    for _, _, comes, does_come in found_pieces:
        pl.when(does_come)(comes.wait_recv)
    found = [joined(found_in, lambda k: (k, part)) for part in range(3)]

    def neighbours(value):
        rows = 4 * node_rows
        return (
            pltpu.roll(value, 1, 0)
            + pltpu.roll(value, rows - 1, 0)
            + pltpu.roll(value, 1, 1)
            + pltpu.roll(value, LANES - 1, 1)
        )

    per_node = float((2 * REACH + 1) ** 2)
    moved = []
    for section in range(2):
        living = nodes[section][2]
        targets = found[:2] if section == 0 else nodes[1][:2]
        stiffness = living * found[2] / per_node if section == 0 else living
        below = 1.0 + stiffness + living * neighbours(living)
        for part in range(2):
            value = living * targets[part]
            for _ in range(ITERS):
                value = (
                    value + stiffness * targets[part] + living * neighbours(living * value)
                ) / below
            moved.append(value[node_rows : 3 * node_rows])
    first = z == 0
    for part in range(2):
        out_ref[0, part] = jnp.where(first, moved[part], moved[2 + part])
        out_ref[1, part] = jnp.where(first, moved[part], moved[part] + moved[2 + part])

    def finish(block, _):
        block_copy(block, z, 1 - z).wait_send()
        return 0

    lax.fori_loop(0, blocks, finish, 0)
    for sent, is_sent, _, _ in pieces + node_pieces + found_pieces:
        pl.when(is_sent)(sent.wait_send)


def working_scratch(node_rows, width):
    return [
        pltpu.VMEM((2, 2, node_rows * HALF, width), jnp.bfloat16),
        pltpu.VMEM((2, node_rows, width), jnp.float32),
        pltpu.VMEM((2, node_rows, width), jnp.float32),
    ]


def match_pair(own, nodes, counts):
    node_cols = nodes.shape[2]
    node_rows = nodes.shape[1] // 2
    width = own.shape[1] + 2 * BLOCK
    blocks = width // BLOCK - 2
    four = np.zeros((LANES, 4, PATCH))
    for node in range(4):
        four[node, node] = 1.0
    constants = [jnp.asarray(t) for t in (bf16(four.reshape(LANES, BLOCK)),) + tables()]
    laid = jnp.pad(nodes, ((0, 0), (0, 0), (ITERS, LANES - ITERS - node_cols)))
    vmem = pl.BlockSpec(memory_space=pltpu.VMEM)
    dma = pltpu.SemaphoreType.DMA
    f32 = jnp.float32
    out = pl.pallas_call(
        functools.partial(pair_kernel, counts, node_rows, node_cols),
        out_shape=jax.ShapeDtypeStruct((2, 2, 2 * node_rows, LANES), f32),
        in_specs=[pl.BlockSpec(memory_space=pl.ANY)] + [vmem] * (1 + len(constants)),
        out_specs=vmem,
        scratch_shapes=working_scratch(node_rows, width)
        + [
            pltpu.VMEM((2, (node_rows + 1) * SPACING, width), jnp.bfloat16),
            pltpu.VMEM((3, node_rows, LANES), f32),
            pltpu.VMEM((3, node_rows, LANES), f32),
            pltpu.VMEM((2, 3, 3, 4 * node_rows, LANES), f32),
            pltpu.VMEM((3, 3, 4 * node_rows, LANES), f32),
            dma,
            dma((12,)),
            dma((12,)),
            dma((blocks,)),
            dma((blocks,)),
            dma,
            dma((17,)),
            dma((17,)),
            dma((12,)),
            dma((12,)),
        ],
        compiler_params=pltpu.CompilerParams(
            vmem_limit_bytes=56 * 1024 * 1024, collective_id=0, has_side_effects=True
        ),
    )(own, laid, *constants)
    out = out[..., ITERS : ITERS + node_cols]
    return out[0], out[1]


def match(strips, offsets):
    node_rows, node_cols = offsets.shape[1:]
    groups = node_cols // 4 + 1
    constants = [jnp.asarray(table) for table in tables()]
    shifted = jnp.pad(offsets.astype(jnp.float32), ((0, 0), (0, 0), (3, 1)))
    spread_offsets = jnp.repeat(shifted, PATCH, axis=2)
    vmem = pl.BlockSpec(memory_space=pltpu.VMEM)
    out = pl.pallas_call(
        functools.partial(plain_kernel, node_rows),
        out_shape=jax.ShapeDtypeStruct((groups, node_rows, 128), jnp.float32),
        in_specs=[vmem] * (2 + len(constants)),
        out_specs=vmem,
        scratch_shapes=working_scratch(node_rows, strips.shape[2]),
        compiler_params=pltpu.CompilerParams(vmem_limit_bytes=56 * 1024 * 1024),
    )(strips, spread_offsets, *constants)
    sums = jnp.transpose(out[:, :, :12].reshape(groups, node_rows, 3, 4), (2, 1, 0, 3))
    sums = sums.reshape(3, node_rows, 4 * groups)[:, :, 3:-1]
    return jnp.stack([sums[2] / sums[0], sums[1] / sums[0], sums[0]], 0)


def beside(value, axis, steps):
    count = lax.axis_size(axis)
    pairs = [(i, i + steps) for i in range(count) if 0 <= i + steps < count]
    return lax.ppermute(value, axis, pairs)


def bordered(field, axis, dim, width):
    length = field.shape[dim]
    before = beside(lax.slice_in_dim(field, length - width, length, axis=dim), axis, 1)
    after = beside(lax.slice_in_dim(field, 0, width, axis=dim), axis, -1)
    return before, after


def neighbour_sum(padded):
    return (
        padded[..., :-2, 1:-1]
        + padded[..., 2:, 1:-1]
        + padded[..., 1:-1, :-2]
        + padded[..., 1:-1, 2:]
    )


def relax(target, stiffness, living):
    fields = jnp.concatenate([target, stiffness[None], living[None]], 0)
    before, after = bordered(fields, "gx", 3, ITERS)
    fields = jnp.concatenate([before, fields, after], 3)
    before, after = bordered(fields, "gy", 2, ITERS)
    fields = jnp.concatenate([before, fields, after], 2)
    target, stiffness, living = fields[:2], fields[2], fields[3]
    moved = living[None] * target
    for _ in range(ITERS):
        pulled = neighbour_sum(living[None] * moved)
        count = neighbour_sum(living)
        inner = (slice(None), slice(1, -1), slice(1, -1))
        target, moved = target[(slice(None),) + inner], moved[(slice(None),) + inner]
        stiffness, living = stiffness[inner], living[inner]
        moved = (moved + stiffness[None] * target + living[None] * pulled) / (
            1.0 + stiffness + living * count
        )[None]
    return moved


def shards(section_pixels, tissue, peak_offsets):
    own = section_pixels[0]
    pixel_rows, pixel_cols = own.shape
    node_rows = pixel_rows // SPACING
    slabs = lax.axis_size("gz")
    offsets = peak_offsets[:, 0].astype(jnp.float32)
    living = tissue.astype(jnp.float32)
    per_node = jnp.float32((2 * REACH + 1) ** 2)

    if (
        slabs == 2
        and node_rows % 16 == 0
        and pixel_cols % BLOCK == 0
        and pixel_cols // SPACING + 2 * ITERS <= LANES
    ):
        counts = tuple(lax.axis_size(axis) for axis in ("gz", "gx", "gy"))
        moved, placed = match_pair(own, jnp.concatenate([offsets, living], 0), counts)
        return moved[:, None], placed[:, None]

    before, after = bordered(own, "gx", 1, LANES)
    own = jnp.concatenate([before, own, after], 1)
    before, after = bordered(own, "gy", 0, MARGIN)
    own = jnp.concatenate([before, own, after], 0)
    strips = jnp.pad(
        jnp.stack([own, beside(own, "gz", -1)], 0), ((0, 0), (0, 0), (BLOCK - LANES, BLOCK - LANES))
    )
    matched = match(strips, offsets)
    moved = relax(matched[:2, None], living * matched[2:] / per_node, living)
    placed = moved
    reach = 1
    while reach < slabs:
        placed = placed + beside(placed, "gz", reach)
        reach *= 2
    return moved, placed


def solution(mesh):
    placed = (P("gz", "gy", "gx"), P("gz", "gy", "gx"), P(None, "gz", "gy", "gx"))
    return jax.shard_map(
        shards,
        mesh=mesh,
        in_specs=placed,
        out_specs=(P(None, "gz", "gy", "gx"), P(None, "gz", "gy", "gx")),
        check_vma=False,
    )
```

```python
import functools
import math

import jax
import jax.numpy as jnp
import ml_dtypes
import numpy as np
from jax import lax
from jax.experimental import pallas as pl
from jax.experimental.pallas import tpu as pltpu
from jax.sharding import PartitionSpec as P

PATCH = 64
REACH = 12
SPACING = 32
ITERS = 3
BOUND = 8
FAR = BOUND + REACH
LAG_ROWS = 48
HALF = PATCH // 2
MARGIN = SPACING // 2
LANES = 128
BLOCK = 256
MESH = pl.DeviceIdType.MESH

sharpness = 32.0
tiny_energy = 1e-06


def bf16(table):
    return np.asarray(table, np.float32).astype(ml_dtypes.bfloat16)


def split(table):
    high = bf16(table)
    return high, bf16(np.asarray(table, np.float32) - high.astype(np.float32))


@functools.lru_cache(None)
def tables():
    n = np.arange(PATCH)
    angle = 2.0 * math.pi * ((n[:, None] * n[None, :]) % PATCH) / PATCH
    cosine, sine = np.cos(angle), np.sin(angle)
    row_table = np.zeros((80, PATCH))
    row_table[:HALF] = cosine[:HALF]
    row_table[HALF:PATCH] = -sine[:HALF]
    row_table[PATCH] = cosine[HALF]
    second = np.zeros((2, 256, 2, 2, 2, PATCH))
    spread = np.zeros((256, 4, PATCH))
    for pair in range(2):
        for q in range(2):
            node = 2 * pair + q
            rows = slice(MARGIN + SPACING * node, MARGIN + SPACING * node + PATCH)
            second[0, rows, pair, 0, q] = cosine.T
            second[0, rows, pair, 1, q] = -sine.T
            second[1, rows, pair, 0, q] = sine.T
            second[1, rows, pair, 1, q] = cosine.T
            spread[rows, node] = 1.0
    lags = np.arange(2 * FAR + 1) - FAR
    lag_angle = 2.0 * math.pi * ((n[:, None] * lags[None, :]) % PATCH) / PATCH
    lag_cos, lag_sin = np.cos(lag_angle), np.sin(lag_angle)
    back = np.zeros((2, 2, PATCH, 2, 2, PATCH))
    for q in range(2):
        back[0, q, :, 0, q, : lags.size] = lag_cos
        back[1, q, :, 0, q, : lags.size] = -lag_sin
        back[0, q, :, 1, q, : lags.size] = lag_sin
        back[1, q, :, 1, q, : lags.size] = lag_cos
    back_high, back_low = split(back.reshape(256, 256))
    fold = np.where(np.arange(HALF) == 0, 1.0, 2.0)[None]
    rows = np.zeros((LAG_ROWS, 2 * HALF))
    rows[: lags.size, :HALF] = fold * lag_cos[:HALF].T
    rows[: lags.size, HALF:] = -fold * lag_sin[:HALF].T
    row_high, row_low = split(rows)
    row_back = np.concatenate([row_high, row_high, row_low], 1)
    gather = np.zeros((4, PATCH, 128))
    lane_lag = np.arange(PATCH) - FAR
    for node in range(4):
        gather[node, :, node] = 1.0
        gather[node, :, 4 + node] = lane_lag
    return (
        bf16(row_table),
        bf16(second.reshape(2, 256, 512)),
        bf16(spread.reshape(256, 256)),
        back_high,
        back_low,
        row_back,
        bf16(gather.reshape(256, 128)),
    )


def match_core(
    node_rows,
    strips_ref,
    row_ref,
    second_ref,
    spread_ref,
    back_high_ref,
    back_low_ref,
    row_back_ref,
    gather_ref,
    half_ref,
    nyquist_ref,
    squares_ref,
    arrive,
    offsets_of,
    give,
):
    f32, b16 = jnp.float32, jnp.bfloat16
    blocks = strips_ref.shape[2] // BLOCK

    def dot(a, b):
        return jnp.dot(a, b, preferred_element_type=f32)

    def parts(value):
        high = value.astype(b16)
        rest = value - high.astype(f32)
        middle = rest.astype(b16)
        return [high.astype(f32), middle.astype(f32), rest - middle.astype(f32)]

    def exact_pair(first, then, table):
        stacked = jnp.concatenate(parts(first) + parts(then), 0).astype(b16)
        got = dot(stacked, table)
        n = first.shape[0]
        terms = [got[k * n : (k + 1) * n] for k in range(6)]
        return terms[0] + terms[1] + terms[2], terms[3] + terms[4] + terms[5]

    def over_rows(block):
        lanes = pl.ds(pl.multiple_of(block * BLOCK, BLOCK), BLOCK)
        for which in range(2):
            for i in range(node_rows):
                rows = strips_ref[which, i * SPACING : i * SPACING + PATCH, lanes]
                got = dot(row_ref[...], rows)
                half_ref[which, 0, i * HALF : (i + 1) * HALF, lanes] = got[:HALF].astype(b16)
                half_ref[which, 1, i * HALF : (i + 1) * HALF, lanes] = got[HALF:PATCH].astype(b16)
                nyquist_ref[which, i : i + 1, lanes] = (
                    got[PATCH : PATCH + 1].astype(b16).astype(f32)
                )
                wide = rows.astype(f32)
                squares_ref[which, i : i + 1, lanes] = jnp.sum(wide * wide, axis=0, keepdims=True)

    row_lag = lax.broadcasted_iota(jnp.int32, (LAG_ROWS, BLOCK), 0) - FAR
    col_lag = (lax.broadcasted_iota(jnp.int32, (LAG_ROWS, BLOCK), 1) & (PATCH - 1)) - FAR
    alternate = jnp.where((row_lag & 1) == 0, 1.0, -1.0).astype(f32)
    row_lag = row_lag.astype(f32)
    col_lag = col_lag.astype(f32)

    def crossed(first, then, pair):
        real, imag = slice(256 * pair, 256 * pair + 128), slice(256 * pair + 128, 256 * pair + 256)
        cross_real = first[:, real] * then[:, real] + first[:, imag] * then[:, imag]
        cross_imag = first[:, real] * then[:, imag] - first[:, imag] * then[:, real]
        return jnp.concatenate([cross_real, cross_imag], 1)

    def over_columns(cross):
        high = cross.astype(b16)
        low = (cross - high.astype(f32)).astype(b16)
        return dot(high, back_high_ref[...]) + dot(low, back_high_ref[...]) + dot(high, back_low_ref[...])

    def four_columns(group):
        lanes = pl.ds(pl.multiple_of((group + 1) * LANES, LANES), BLOCK)
        spectra = []
        for which in range(2):
            spectra.append(
                dot(half_ref[which, 0, :, lanes], second_ref[0])
                + dot(half_ref[which, 1, :, lanes], second_ref[1])
            )
        both = jnp.concatenate([nyquist_ref[0, :, lanes], nyquist_ref[1, :, lanes]], 0)
        edges = dot(both.astype(b16), second_ref[0])
        energies = exact_pair(squares_ref[0, :, lanes], squares_ref[1, :, lanes], spread_ref[...])
        scale = (sharpness / (PATCH * PATCH)) / jnp.sqrt(energies[0] * energies[1] + tiny_energy)
        main = node_rows * HALF
        back = over_columns(
            jnp.concatenate(
                [crossed(spectra[0], spectra[1], pair) for pair in range(2)]
                + [crossed(edges[:node_rows], edges[node_rows:], pair) for pair in range(2)],
                0,
            )
        )
        columns = [back[:main], back[main : 2 * main]]
        edge_columns = jnp.concatenate(
            [back[2 * main : 2 * main + node_rows, :128], back[2 * main + node_rows :, :128]], 1
        )
        row_offset, col_offset = offsets_of(group)
        totals, row_totals = [], []
        for i in range(node_rows):
            rows = slice(i * HALF, (i + 1) * HALF)
            field = jnp.concatenate(
                [
                    jnp.concatenate([columns[0][rows, :128], columns[1][rows, :128]], 1),
                    jnp.concatenate([columns[0][rows, 128:], columns[1][rows, 128:]], 1),
                ],
                0,
            )
            high = field.astype(b16)
            low = (field - high.astype(f32)).astype(b16)
            found = dot(row_back_ref[...], jnp.concatenate([high, low, high], 0))
            found = found + alternate * edge_columns[i : i + 1]
            in_rows = jnp.abs(row_lag - row_offset[i : i + 1]) <= REACH
            in_cols = jnp.abs(col_lag[:1] - col_offset[i : i + 1]) <= REACH
            weights = jnp.where(in_rows, jnp.exp(found * scale[i : i + 1]), 0.0)
            totals.append(jnp.where(in_cols, jnp.sum(weights, axis=0, keepdims=True), 0.0))
            row_totals.append(
                jnp.where(in_cols, jnp.sum(weights * row_lag, axis=0, keepdims=True), 0.0)
            )
        plain, by_row = exact_pair(
            jnp.concatenate(totals, 0), jnp.concatenate(row_totals, 0), gather_ref[...]
        )
        few = lax.broadcasted_iota(jnp.int32, (node_rows, LANES), 1)
        give(group, plain + pltpu.roll(jnp.where(few < 4, by_row, 0.0), 8, 1))

    over_rows(0)

    def one(block, _):
        arrive(block)
        over_rows(block + 1)
        four_columns(2 * block)
        four_columns(2 * block + 1)
        return 0

    lax.fori_loop(0, blocks - 2, one, 0)
    over_rows(blocks - 1)
    four_columns(2 * (blocks - 2))


def plain_kernel(node_rows, strips_ref, offsets_ref, *refs):
    tables_of, (out_ref, *scratch) = refs[:7], refs[7:]

    def offsets_of(group):
        here = pl.ds(pl.multiple_of(group * BLOCK, BLOCK), BLOCK)
        return offsets_ref[0, :, here], offsets_ref[1, :, here]

    def give(group, sums):
        out_ref[group] = sums

    match_core(node_rows, strips_ref, *tables_of, *scratch, lambda block: None, offsets_of, give)


def pair_kernel(counts, node_rows, node_cols, own_ref, nodes_ref, four_ref, *refs):
    tables_of, (out_ref, *refs) = refs[:7], refs[7:]
    work, (
        strips_ref,
        sums_ref,
        ours_ref,
        nodes_in,
        found_in,
        local_sem,
        send_sem,
        recv_sem,
        main_send,
        main_recv,
        node_sem,
        node_send,
        node_recv,
        found_send,
        found_recv,
    ) = refs[:3], refs[3:]
    f32 = jnp.float32
    slabs, columns, rows_of = counts
    z, x, y = lax.axis_index("gz"), lax.axis_index("gx"), lax.axis_index("gy")
    height, width = own_ref.shape
    main = node_rows * SPACING + MARGIN
    strip = main + MARGIN
    zero = jnp.bfloat16(0)
    strips_ref[:, :MARGIN, :] = jnp.full((2, MARGIN, width + 2 * BLOCK), zero)
    strips_ref[:, main:, :] = jnp.full((2, MARGIN, width + 2 * BLOCK), zero)
    strips_ref[:, :, :BLOCK] = jnp.full((2, strip, BLOCK), zero)
    strips_ref[:, :, BLOCK + width :] = jnp.full((2, strip, BLOCK), zero)
    nodes_in[...] = jnp.zeros(nodes_in.shape, f32)
    found_in[...] = jnp.zeros(found_in.shape, f32)
    sums_ref[...] = jnp.zeros(sums_ref.shape, f32)

    def rows_at(start, size):
        return pl.ds(pl.multiple_of(start, MARGIN), size)

    def source_main(slab):
        return rows_at(slab * (height - main), main)

    def landed_main(slab):
        return rows_at((1 - slab) * MARGIN, main)

    def source_edge(slab):
        return rows_at((1 - slab) * (height - MARGIN), MARGIN)

    def landed_edge(slab):
        return rows_at(slab * main, MARGIN)

    left, right, centre = pl.ds(BLOCK - LANES, LANES), pl.ds(BLOCK + width, LANES), pl.ds(BLOCK, width)
    sides = (
        (1, pl.ds(width - LANES, LANES), left),
        (-1, pl.ds(0, LANES), right),
        (0, pl.ds(0, width), centre),
    )

    def inside(place, count):
        return (place >= 0) & (place < count)

    pieces = []
    for other in range(2):
        slab = z if other == 0 else 1 - z
        for vertical in range(2):
            for number, (shift, source_lanes, landed_lanes) in enumerate(sides):
                if shift == 0 and vertical == 0:
                    continue
                slot = (other * 2 + vertical) * 3 + number
                down = (1 - 2 * slab) * vertical
                source = (source_edge if vertical else source_main)(slab)
                landed = (landed_edge if vertical else landed_main)(slab)
                sent = pltpu.make_async_remote_copy(
                    src_ref=own_ref.at[source, source_lanes],
                    dst_ref=strips_ref.at[z, landed, landed_lanes],
                    send_sem=send_sem.at[slot],
                    recv_sem=recv_sem.at[slot],
                    device_id=(slab, x + shift, y + down),
                    device_id_type=MESH,
                )
                is_sent = inside(x + shift, columns) & inside(y + down, rows_of)
                mine = (landed_edge if vertical else landed_main)(z)
                up = (1 - 2 * z) * vertical
                giver = (slab, x - shift, y - up)
                comes = pltpu.make_async_remote_copy(
                    src_ref=own_ref.at[source, source_lanes],
                    dst_ref=strips_ref.at[slab, mine, landed_lanes],
                    send_sem=send_sem.at[slot],
                    recv_sem=recv_sem.at[slot],
                    device_id=giver,
                    device_id_type=MESH,
                )
                does_come = inside(x - shift, columns) & inside(y - up, rows_of)
                pieces.append((sent, is_sent, comes, does_come))

    def node_source(dy):
        if dy == 0:
            return pl.ds(0, 2 * node_rows)
        return pl.ds(node_rows if dy == 1 else 0, node_rows)

    def node_landed(dy):
        if dy == 0:
            return pl.ds(node_rows, 2 * node_rows)
        return pl.ds(0 if dy == 1 else 3 * node_rows, node_rows)

    around = [
        (other, dx, dy)
        for other in range(2)
        for dx in (-1, 0, 1)
        for dy in (-1, 0, 1)
        if (other, dx, dy) != (0, 0, 0)
    ]
    node_pieces = []
    for slot, (other, dx, dy) in enumerate(around):
        slab = z if other == 0 else 1 - z
        copies = []
        for section, device in ((z, (slab, x + dx, y + dy)), (slab, (slab, x - dx, y - dy))):
            copies.append(
                pltpu.make_async_remote_copy(
                    src_ref=nodes_ref.at[:, node_source(dy)],
                    dst_ref=nodes_in.at[section, 1 - dx, :, node_landed(dy)],
                    send_sem=node_send.at[slot],
                    recv_sem=node_recv.at[slot],
                    device_id=device,
                    device_id_type=MESH,
                )
            )
        goes = inside(x + dx, columns) & inside(y + dy, rows_of)
        comes = inside(x - dx, columns) & inside(y - dy, rows_of)
        node_pieces.append((copies[0], goes, copies[1], comes))

    found_pieces = []
    for other in range(2):
        for dx in (-1, 0, 1):
            for vertical in range(2):
                if (other, dx, vertical) == (0, 0, 0):
                    continue
                slot = (other * 3 + dx + 1) * 2 + vertical
                slab = z if other == 0 else 1 - z
                copies = []
                for finder, sign in ((z, 1), (slab, -1)):
                    down = (2 * finder - 1) * vertical
                    row = (1 + finder) * node_rows if vertical == 0 else 3 * (1 - finder) * node_rows
                    copies.append(
                        (
                            pltpu.make_async_remote_copy(
                                src_ref=ours_ref,
                                dst_ref=found_in.at[
                                    1 - dx, :, pl.ds(pl.multiple_of(row, node_rows), node_rows)
                                ],
                                send_sem=found_send.at[slot],
                                recv_sem=found_recv.at[slot],
                                device_id=(slab, x + sign * dx, y + sign * down),
                                device_id_type=MESH,
                            ),
                            inside(x + sign * dx, columns) & inside(y + sign * down, rows_of),
                        )
                    )
                found_pieces.append(copies[0] + copies[1])

    barrier = pltpu.get_barrier_semaphore()
    targets = jnp.int32(0)
    for other, dx, dy in around:
        there = inside(x + dx, columns) & inside(y + dy, rows_of)

        @pl.when(there)
        def _():
            pl.semaphore_signal(
                barrier,
                inc=1,
                device_id=(z if other == 0 else 1 - z, x + dx, y + dy),
                device_id_type=MESH,
            )

        targets = targets + there.astype(jnp.int32)
    own_nodes = pltpu.make_async_copy(
        nodes_ref, nodes_in.at[z, 1, :, node_landed(0)], node_sem
    )
    own_nodes.start()
    local = pltpu.make_async_copy(
        own_ref.at[source_main(z)], strips_ref.at[z, landed_main(z), centre], local_sem
    )
    local.start()
    pl.semaphore_wait(barrier, targets)

    for sent, is_sent, _, _ in pieces + node_pieces:
        pl.when(is_sent)(sent.start)

    def block_copy(block, section, slab):
        at = pl.multiple_of(block * BLOCK, BLOCK)
        return pltpu.make_async_remote_copy(
            src_ref=own_ref.at[source_main(1 - z), pl.ds(at, BLOCK)],
            dst_ref=strips_ref.at[section, landed_main(slab), pl.ds(BLOCK + at, BLOCK)],
            send_sem=main_send.at[block],
            recv_sem=main_recv.at[block],
            device_id=(1 - z, x, y),
            device_id_type=MESH,
        )

    blocks = width // BLOCK

    def start(block, _):
        block_copy(block, z, 1 - z).start()
        return 0

    lax.fori_loop(0, blocks, start, 0)
    local.wait()
    own_nodes.wait()
    for _, _, comes, does_come in pieces + node_pieces:
        pl.when(does_come)(comes.wait_recv)

    upper = pl.ds(pl.multiple_of((1 + z) * node_rows, node_rows), node_rows)

    def offsets_of(group):
        return [
            jnp.dot(
                pltpu.roll(nodes_in[0, 1, part, upper, :], lax.rem(LANES - 4 * group, LANES), 1).astype(
                    jnp.bfloat16
                ),
                four_ref[...],
                preferred_element_type=f32,
            )
            for part in range(2)
        ]

    few = lax.broadcasted_iota(jnp.int32, (node_rows, LANES), 1)

    def give(group, sums):
        for part in range(3):
            one = jnp.where((few >= 4 * part) & (few < 4 * part + 4), sums, 0.0)
            sums_ref[part] += pltpu.roll(one, lax.rem(4 * group - 4 * part + LANES, LANES), 1)

    match_core(
        node_rows,
        strips_ref,
        *tables_of,
        *work,
        lambda block: block_copy(block, 1 - z, z).wait_recv(),
        offsets_of,
        give,
    )
    total = sums_ref[0]
    held = (few >= ITERS) & (few < ITERS + node_cols)
    ours_ref[0] = jnp.where(held, sums_ref[2] / total, 0.0)
    ours_ref[1] = jnp.where(held, sums_ref[1] / total, 0.0)
    ours_ref[2] = jnp.where(held, total, 0.0)
    for sent, is_sent, _, _ in found_pieces:
        pl.when(is_sent)(sent.start)
    found_in[1, :, upper, :] = ours_ref[...]

    lane = lax.broadcasted_iota(jnp.int32, (4 * node_rows, LANES), 1)

    def joined(ref, at):
        before = pltpu.roll(ref[at(0)], LANES - node_cols, 1)
        after = pltpu.roll(ref[at(2)], node_cols, 1)
        value = jnp.where(lane < ITERS, before, ref[at(1)])
        value = jnp.where(lane < ITERS + node_cols, value, after)
        return jnp.where(lane < 2 * ITERS + node_cols, value, 0.0)

    nodes = [[joined(nodes_in, lambda k: (s, k, part)) for part in range(3)] for s in range(2)]
    for _, _, comes, does_come in found_pieces:
        pl.when(does_come)(comes.wait_recv)
    found = [joined(found_in, lambda k: (k, part)) for part in range(3)]

    def neighbours(value):
        rows = 4 * node_rows
        return (
            pltpu.roll(value, 1, 0)
            + pltpu.roll(value, rows - 1, 0)
            + pltpu.roll(value, 1, 1)
            + pltpu.roll(value, LANES - 1, 1)
        )

    per_node = float((2 * REACH + 1) ** 2)
    moved = []
    for section in range(2):
        living = nodes[section][2]
        targets = found[:2] if section == 0 else nodes[1][:2]
        stiffness = living * found[2] / per_node if section == 0 else living
        below = 1.0 + stiffness + living * neighbours(living)
        for part in range(2):
            value = living * targets[part]
            for _ in range(ITERS):
                value = (
                    value + stiffness * targets[part] + living * neighbours(living * value)
                ) / below
            moved.append(value[node_rows : 3 * node_rows])
    first = z == 0
    for part in range(2):
        out_ref[0, part] = jnp.where(first, moved[part], moved[2 + part])
        out_ref[1, part] = jnp.where(first, moved[part], moved[part] + moved[2 + part])

    def finish(block, _):
        block_copy(block, z, 1 - z).wait_send()
        return 0

    lax.fori_loop(0, blocks, finish, 0)
    for sent, is_sent, _, _ in pieces + node_pieces + found_pieces:
        pl.when(is_sent)(sent.wait_send)


def working_scratch(node_rows, width):
    return [
        pltpu.VMEM((2, 2, node_rows * HALF, width), jnp.bfloat16),
        pltpu.VMEM((2, node_rows, width), jnp.float32),
        pltpu.VMEM((2, node_rows, width), jnp.float32),
    ]


def match_pair(own, nodes, counts):
    node_cols = nodes.shape[2]
    node_rows = nodes.shape[1] // 2
    width = own.shape[1] + 2 * BLOCK
    blocks = width // BLOCK - 2
    four = np.zeros((LANES, 4, PATCH))
    for node in range(4):
        four[node, node] = 1.0
    constants = [jnp.asarray(t) for t in (bf16(four.reshape(LANES, BLOCK)),) + tables()]
    laid = jnp.pad(nodes, ((0, 0), (0, 0), (ITERS, LANES - ITERS - node_cols)))
    vmem = pl.BlockSpec(memory_space=pltpu.VMEM)
    dma = pltpu.SemaphoreType.DMA
    f32 = jnp.float32
    out = pl.pallas_call(
        functools.partial(pair_kernel, counts, node_rows, node_cols),
        out_shape=jax.ShapeDtypeStruct((2, 2, 2 * node_rows, LANES), f32),
        in_specs=[pl.BlockSpec(memory_space=pl.ANY)] + [vmem] * (1 + len(constants)),
        out_specs=vmem,
        scratch_shapes=working_scratch(node_rows, width)
        + [
            pltpu.VMEM((2, (node_rows + 1) * SPACING, width), jnp.bfloat16),
            pltpu.VMEM((3, node_rows, LANES), f32),
            pltpu.VMEM((3, node_rows, LANES), f32),
            pltpu.VMEM((2, 3, 3, 4 * node_rows, LANES), f32),
            pltpu.VMEM((3, 3, 4 * node_rows, LANES), f32),
            dma,
            dma((12,)),
            dma((12,)),
            dma((blocks,)),
            dma((blocks,)),
            dma,
            dma((17,)),
            dma((17,)),
            dma((12,)),
            dma((12,)),
        ],
        compiler_params=pltpu.CompilerParams(
            vmem_limit_bytes=56 * 1024 * 1024, collective_id=0, has_side_effects=True
        ),
    )(own, laid, *constants)
    out = out[..., ITERS : ITERS + node_cols]
    return out[0], out[1]


def match(strips, offsets):
    node_rows, node_cols = offsets.shape[1:]
    groups = node_cols // 4 + 1
    constants = [jnp.asarray(table) for table in tables()]
    shifted = jnp.pad(offsets.astype(jnp.float32), ((0, 0), (0, 0), (3, 1)))
    spread_offsets = jnp.repeat(shifted, PATCH, axis=2)
    vmem = pl.BlockSpec(memory_space=pltpu.VMEM)
    out = pl.pallas_call(
        functools.partial(plain_kernel, node_rows),
        out_shape=jax.ShapeDtypeStruct((groups, node_rows, 128), jnp.float32),
        in_specs=[vmem] * (2 + len(constants)),
        out_specs=vmem,
        scratch_shapes=working_scratch(node_rows, strips.shape[2]),
        compiler_params=pltpu.CompilerParams(vmem_limit_bytes=56 * 1024 * 1024),
    )(strips, spread_offsets, *constants)
    sums = jnp.transpose(out[:, :, :12].reshape(groups, node_rows, 3, 4), (2, 1, 0, 3))
    sums = sums.reshape(3, node_rows, 4 * groups)[:, :, 3:-1]
    return jnp.stack([sums[2] / sums[0], sums[1] / sums[0], sums[0]], 0)


def beside(value, axis, steps):
    count = lax.axis_size(axis)
    pairs = [(i, i + steps) for i in range(count) if 0 <= i + steps < count]
    return lax.ppermute(value, axis, pairs)


def bordered(field, axis, dim, width):
    length = field.shape[dim]
    before = beside(lax.slice_in_dim(field, length - width, length, axis=dim), axis, 1)
    after = beside(lax.slice_in_dim(field, 0, width, axis=dim), axis, -1)
    return before, after


def neighbour_sum(padded):
    return (
        padded[..., :-2, 1:-1]
        + padded[..., 2:, 1:-1]
        + padded[..., 1:-1, :-2]
        + padded[..., 1:-1, 2:]
    )


def relax(target, stiffness, living):
    fields = jnp.concatenate([target, stiffness[None], living[None]], 0)
    before, after = bordered(fields, "gx", 3, ITERS)
    fields = jnp.concatenate([before, fields, after], 3)
    before, after = bordered(fields, "gy", 2, ITERS)
    fields = jnp.concatenate([before, fields, after], 2)
    target, stiffness, living = fields[:2], fields[2], fields[3]
    moved = living[None] * target
    for _ in range(ITERS):
        pulled = neighbour_sum(living[None] * moved)
        count = neighbour_sum(living)
        inner = (slice(None), slice(1, -1), slice(1, -1))
        target, moved = target[(slice(None),) + inner], moved[(slice(None),) + inner]
        stiffness, living = stiffness[inner], living[inner]
        moved = (moved + stiffness[None] * target + living[None] * pulled) / (
            1.0 + stiffness + living * count
        )[None]
    return moved


def shards(section_pixels, tissue, peak_offsets):
    own = section_pixels[0]
    pixel_rows, pixel_cols = own.shape
    node_rows = pixel_rows // SPACING
    slabs = lax.axis_size("gz")
    offsets = peak_offsets[:, 0].astype(jnp.float32)
    living = tissue.astype(jnp.float32)
    per_node = jnp.float32((2 * REACH + 1) ** 2)

    if (
        slabs == 2
        and node_rows % 16 == 0
        and pixel_cols % BLOCK == 0
        and pixel_cols // SPACING + 2 * ITERS <= LANES
    ):
        counts = tuple(lax.axis_size(axis) for axis in ("gz", "gx", "gy"))
        moved, placed = match_pair(own, jnp.concatenate([offsets, living], 0), counts)
        return moved[:, None], placed[:, None]

    before, after = bordered(own, "gx", 1, LANES)
    own = jnp.concatenate([before, own, after], 1)
    before, after = bordered(own, "gy", 0, MARGIN)
    own = jnp.concatenate([before, own, after], 0)
    strips = jnp.pad(
        jnp.stack([own, beside(own, "gz", -1)], 0), ((0, 0), (0, 0), (BLOCK - LANES, BLOCK - LANES))
    )
    matched = match(strips, offsets)
    moved = relax(matched[:2, None], living * matched[2:] / per_node, living)
    placed = moved
    reach = 1
    while reach < slabs:
        placed = placed + beside(placed, "gz", reach)
        reach *= 2
    return moved, placed


def solution(mesh):
    placed = (P("gz", "gy", "gx"), P("gz", "gy", "gx"), P(None, "gz", "gy", "gx"))
    return jax.shard_map(
        shards,
        mesh=mesh,
        in_specs=placed,
        out_specs=(P(None, "gz", "gy", "gx"), P(None, "gz", "gy", "gx")),
        check_vma=False,
    )
```
